128 devices in a mesh: chan: 16 (over y, x), tm: 8 (over z, core).
Axes of the slice: x: 4, y: 4, z: 4, core: 2. Of those that a mesh axis runs over, the one named last changes fastest.
Arguments:
- samples: bfloat16 [256, 192, 4096], P('chan', 'tm'), may hold values from -6 to 6
- taps: float32 [16, 4096], replicated, may hold values from -1.5 to 1.5
- block_tile: int32 [120], replicated, may hold values from 0 to 15, as said below
- tile_slots: int32 [16], replicated, may hold values from 0 to 15, as said below
- kern_u: bfloat16 [16, 30720], replicated, may hold values from -1.1953125 to 1.1953125
- kern_v: bfloat16 [16, 30720], replicated, may hold values from -1.1953125 to 1.1953125
Outputs:
- uv_grid: float32 [16, 2048, 2, 256], P('tm', 'chan')
The draws below stay inside these ranges and needn't reach their ends.
Inputs may be any that keep to these rules, and one draw needn't show every extreme that they name: `block_tile`: A tile's owner is (its position in tile_slots) // 2. The blocks that fall in the tiles of one owner are at most 30; in every draw one owner has exactly 30. `tile_slots`: each tile number stands once.
All inputs are finite; a program needn't handle non-finite values.
Results may differ from the reference program's by a relative error of at most 0.0077.
Values may be sent and summed in bfloat16 or wider, within the bound.
No kernel may reach another device: no remote copies, remote signals or barrier semaphores. Data moves between devices by JAX's collectives and lax.ppermute only.
A program may use at most 192 MiB of HBM per device.

```python
import math
import jax
import jax.numpy as jnp
import numpy as np
from jax import lax

S = 256
L = 4096
TAPS = 16
SBLK = 16
GRID = 16
TILES_DEV = 2
F = 2048
GROUP = 16
FRAMES = 192
NSB = 16
NBLK = 120
NBASE = 30720
NTILES = 16
CAP = 30


def routing_tables(key):
    keys = jax.random.split(jax.random.fold_in(key, 7), 5)
    owners = NTILES // TILES_DEV
    slot_tile = jax.random.permutation(keys[0], NTILES).astype(jnp.int32)
    heavy = jax.random.randint(keys[1], (), 0, owners).astype(jnp.int32)
    block_order = jax.random.permutation(keys[2], NBLK).astype(jnp.int32)
    rest_slots = jax.random.permutation(keys[3], (owners - 1) * CAP)[:NBLK - CAP].astype(jnp.int32)
    rest_rank = rest_slots // CAP
    rest_owner = rest_rank + (rest_rank >= heavy).astype(jnp.int32)
    owner_by_pos = jnp.concatenate([jnp.full((CAP,), heavy, jnp.int32), rest_owner])
    owner_of_block = jnp.zeros((NBLK,), jnp.int32).at[block_order].set(owner_by_pos)
    within = jax.random.randint(keys[4], (NBLK,), 0, TILES_DEV).astype(jnp.int32)
    block_tile = slot_tile[owner_of_block * TILES_DEV + within]
    return (block_tile.astype(jnp.int32), slot_tile)


def draw_block_tile(key, part):
    return routing_tables(key)[0]


def draw_tile_slots(key, part):
    return routing_tables(key)[1]


def block_levels(own_key, shape, cuts, low, top_value):
    level = 1.0
    for dim, blocks in cuts:
        draws = jax.random.uniform(jax.random.fold_in(jax.random.fold_in(own_key, 6), dim), (blocks,), jnp.float32, low / len(cuts), top_value / len(cuts))
        level = level * jnp.repeat(jnp.exp(draws), shape[dim] // blocks).reshape((-1,) + (1,) * (len(shape) - 1 - dim))
    return level


def centred(key, dims, deviation, limit, cuts=(), held_as=jnp.bfloat16):
    entries = jax.random.normal(key, dims, jnp.float32) * deviation
    if len(cuts) > 0:
        entries = block_levels(key, dims, cuts, -0.22, 0.18) * entries
    return jnp.clip(entries, min=-limit, max=limit).astype(held_as)


def setup_inputs(seed: int = 0) -> dict:
    key_of = jax.random.split(jax.random.key(seed), 7)
    samples = centred(key_of[0], (S, FRAMES, L), 1.0, 6.0, ((0, 16), (1, 8)))
    taps = centred(key_of[1], (TAPS, L), 0.25, 1.5, (), jnp.float32)
    block_tile = draw_block_tile(jax.random.fold_in(key_of[6], 71), 0)
    tile_slots = draw_tile_slots(jax.random.fold_in(key_of[6], 71), 0)
    kern_u = centred(key_of[4], (GRID, NBASE), 0.2, 1.1953125)
    kern_v = centred(key_of[5], (GRID, NBASE), 0.2, 1.1953125)
    return {"samples": samples, "taps": taps, "block_tile": block_tile, "tile_slots": tile_slots, "kern_u": kern_u, "kern_v": kern_v}


highest = lax.Precision.HIGHEST

def block_pairs(block_total):
    left_list = []
    right_list = []
    for p in range(block_total):
        for q in range(p + 1, block_total):
            left_list.append(p)
            right_list.append(q)
    return (np.array(left_list, dtype=np.int32), np.array(right_list, dtype=np.int32))

def reference(samples, taps, block_tile, tile_slots, kern_u, kern_v):
    positions = jnp.arange(L, dtype=jnp.int32)[:, None]
    channels = jnp.arange(F, dtype=jnp.int32)[None, :]
    phase_int = positions * channels % L
    phase_angle = phase_int.astype(jnp.float32) * (2.0 * math.pi / L)
    cosine = jnp.cos(phase_angle).astype(jnp.bfloat16)
    sine_neg = (-jnp.sin(phase_angle)).astype(jnp.bfloat16)
    dft_table = jnp.concatenate([cosine, sine_neg], axis=1).astype(jnp.float32)
    dft_scale = 1.0 / math.sqrt(L)

    def channelize(station_group):
        padded = jnp.concatenate([jnp.zeros((SBLK, TAPS - 1, L), station_group.dtype), station_group], axis=1)
        filtered = jnp.zeros((SBLK, FRAMES, L), jnp.float32)
        for tap_index in range(TAPS):
            offset = TAPS - 1 - tap_index
            filtered = filtered + taps[tap_index] * padded[:, offset:offset + FRAMES].astype(jnp.float32)
        rounded = lax.optimization_barrier(filtered.astype(jnp.bfloat16))
        rows_in = rounded.astype(jnp.float32).reshape(SBLK * FRAMES, L)
        spectrum = jnp.dot(rows_in, dft_table, precision=highest) * dft_scale
        return spectrum.astype(jnp.bfloat16).reshape(SBLK, FRAMES, 2, F)
    spectra = lax.map(channelize, samples.reshape(NSB, SBLK, FRAMES, L)).reshape(S, FRAMES, 2, F)
    left_idx, right_idx = block_pairs(NSB)
    u_cols = kern_u.astype(jnp.float32).reshape(GRID, NBLK, SBLK * SBLK).transpose(1, 2, 0)
    v_cols = kern_v.astype(jnp.float32).reshape(GRID, NBLK, SBLK * SBLK).transpose(1, 2, 0)
    kernel = (u_cols[:, :, :, None] * v_cols[:, :, None, :]).reshape(NBLK, SBLK * SBLK, GRID * GRID)
    kernel_wide = kernel.astype(jnp.bfloat16).astype(jnp.float32)
    tile_match = (block_tile[:, None] == tile_slots[None, :]).astype(jnp.float32)
    vis_scale = 1.0 / math.sqrt(FRAMES)

    def correlate(chan_start):
        chan_slice = lax.dynamic_slice_in_dim(spectra, chan_start, GROUP, axis=3).astype(jnp.float32)
        swapped = jnp.concatenate([chan_slice[:, :, 1:2], -chan_slice[:, :, 0:1]], axis=2)
        real_part = jnp.einsum('ibcg,jbcg->gij', chan_slice, chan_slice, precision=highest) * vis_scale
        imag_part = jnp.einsum('ibcg,jbcg->gij', swapped, chan_slice, precision=highest) * vis_scale
        visibility = jnp.stack([real_part, imag_part], axis=1).reshape(GROUP, 2, NSB, SBLK, NSB, SBLK)
        visibility = visibility[:, :, left_idx, :, right_idx, :]
        blocks = visibility.reshape(NBLK, GROUP, 2, SBLK * SBLK).astype(jnp.bfloat16).astype(jnp.float32)
        per_block = jnp.einsum('mgce,mel->mgcl', blocks, kernel_wide, precision=highest)
        return jnp.einsum('mgcl,ms->sgcl', per_block, tile_match, precision=highest)
    starts = jnp.arange(F // GROUP, dtype=jnp.int32) * GROUP
    tile_grids = lax.map(correlate, starts)
    return tile_grids.transpose(1, 0, 2, 3, 4).reshape(NTILES, F, 2, GRID * GRID)
```

```python
import functools
import math

import jax
import jax.numpy as jnp
import ml_dtypes
import numpy as np
from jax import lax
from jax.experimental import pallas as pl
from jax.experimental.pallas import tpu as pltpu
from jax.sharding import PartitionSpec as P

SBLK = 16
GRID = 16
RADIX = 16
HALO = 16
LANES = 128
BF = jnp.bfloat16
F32 = jnp.float32
NT = (((1,), (1,)), ((), ()))
TN = (((0,), (0,)), ((), ()))


def dft_tables(length):
    span = length // RADIX
    place = np.arange(span)[None, :]
    dest = np.arange(length // (2 * RADIX))[:, None]

    def table(low):
        angle = (place * (low + RADIX * dest) % length) * (2.0 * np.pi / length)
        c, s = np.cos(angle), np.sin(angle)
        sign = -1.0 if low > RADIX // 2 else 1.0
        return np.block([[c, sign * s], [-s, sign * c]]) / math.sqrt(length)

    pairs = np.stack(
        [np.concatenate([table(k), table(RADIX - k)], axis=0) for k in range(1, RADIX // 2)]
    )
    ends = np.stack([table(0)[:, :span], table(RADIX // 2)[:, :span]])
    return pairs.astype(ml_dtypes.bfloat16), ends.astype(ml_dtypes.bfloat16)


def real_dft(x):
    n = len(x)
    if n == 2:
        return [(x[0] + x[1], None), (x[0] - x[1], None)]
    even, odd = real_dft(x[0::2]), real_dft(x[1::2])
    out = [None] * (n // 2 + 1)
    for k in range(n // 4 + 1):
        er, ei = even[k]
        dr, di = odd[k]
        if k == 0:
            out[0], out[n // 2] = (er + dr, None), (er - dr, None)
        elif k == n // 4:
            out[k] = (er, -dr)
        else:
            c, s = math.cos(2 * math.pi * k / n), math.sin(2 * math.pi * k / n)
            if 8 * k == n:
                tr, ti = (dr + di) * c, (di - dr) * c
            else:
                tr, ti = dr * c + di * s, di * c - dr * s
            out[k] = (er + tr, ei + ti)
            out[n // 2 - k] = (er - tr, ti - ei)
    return out


def channelize_kernel(
    x_ref, halo_ref, taps_ref, pairs_ref, ends_ref, out_ref, xs, filt, low, turned
):
    stations, frames, length = x_ref.shape
    taps = taps_ref.shape[0]
    span = length // RADIX
    rows = stations * frames
    dests = length // (2 * RADIX)

    for half in range(span // LANES):

        def fir(tile, _):
            at = pl.ds(pl.multiple_of(tile * span + half * LANES, LANES), LANES)
            for s in range(stations):
                xs[pl.ds(s, HALO, stride=stations), :] = halo_ref[s, :, at].astype(F32)
                xs[pl.ds(HALO * stations + s, frames, stride=stations), :] = x_ref[
                    s, :, at
                ].astype(F32)
            weights = [taps_ref[pl.ds(k, 1), at] for k in range(taps)]
            sums = {}
            for step in range(HALO - taps + 1, HALO + frames):
                x = xs[step * stations : (step + 1) * stations, :]
                for k in range(taps - 1, -1, -1):
                    b = step - HALO + k
                    if 0 <= b < frames:
                        term = weights[k] * x
                        sums[b] = sums[b] + term if b in sums else term
                if step >= HALO:
                    b = step - HALO
                    filt[tile, b * stations : (b + 1) * stations, :] = sums.pop(b).astype(BF)
            return 0

        lax.fori_loop(0, RADIX, fir, 0)

        def butterfly(b, _):
            at = pl.ds(pl.multiple_of(b * stations, stations), stations)
            parts = real_dft([filt[tile, at, :].astype(F32) for tile in range(RADIX)])
            to = slice(half * LANES, (half + 1) * LANES)
            for k, (re, im) in enumerate(parts):
                low[k, at, to] = re.astype(BF)
                if im is not None:
                    low[RADIX // 2 + k, at, to] = im.astype(BF)
            return 0

        lax.fori_loop(0, frames, butterfly, 0)

    def keep(channel, part, value):
        for tile in range(rows // LANES):
            turned[
                tile, pl.ds(channel * 2 + part, dests, stride=2 * RADIX), :
            ] = value[:, tile * LANES : (tile + 1) * LANES]

    for end in range(2):
        z = lax.dot_general(
            ends_ref[end], low[end * (RADIX // 2)], NT, preferred_element_type=F32
        )
        for part in range(2):
            keep(end * (RADIX // 2), part, z[part * dests : (part + 1) * dests])

    def pair(k, _):
        spectrum = jnp.concatenate([low[k], low[RADIX // 2 + k]], axis=1)
        for mirrored in range(2):
            z = lax.dot_general(
                pairs_ref[k - 1, mirrored * 2 * dests : (mirrored + 1) * 2 * dests, :],
                spectrum,
                NT,
                preferred_element_type=F32,
            )
            channel = RADIX - k if mirrored else k
            for part in range(2):
                keep(channel, part, z[part * dests : (part + 1) * dests])
        return 0

    lax.fori_loop(1, RADIX // 2, pair, 0)

    def give(d, _):
        at = pl.ds(pl.multiple_of(d * 2 * RADIX, 2 * RADIX), 2 * RADIX)
        for tile in range(rows // LANES):
            out_ref[d, :, tile * LANES : (tile + 1) * LANES] = turned[tile, at, :].astype(BF)
        return 0

    lax.fori_loop(0, dests, give, 0, unroll=4)


def channelize(samples, halo, taps):
    stations, frames, length = samples.shape
    rows = stations * frames
    span = length // RADIX
    dests = length // (2 * RADIX)
    pairs, ends = dft_tables(length)
    whole = pl.BlockSpec(memory_space=pltpu.VMEM)
    return pl.pallas_call(
        channelize_kernel,
        out_shape=jax.ShapeDtypeStruct((dests, 2 * RADIX, rows), BF),
        in_specs=[whole] * 5,
        out_specs=whole,
        scratch_shapes=[
            pltpu.VMEM(((HALO + frames) * stations, LANES), F32),
            pltpu.VMEM((RADIX, rows, LANES), BF),
            pltpu.VMEM((RADIX, rows, span), BF),
            pltpu.VMEM((rows // LANES, dests * 2 * RADIX, LANES), F32),
        ],
        compiler_params=pltpu.CompilerParams(vmem_limit_bytes=50 << 20),
        name="channelize",
    )(samples, halo, taps, jnp.asarray(pairs), jnp.asarray(ends))


def swap_groups(v):
    lane = lax.broadcasted_iota(jnp.int32, v[0].shape, 1)
    v = list(v)
    for bit in (1, 2, 4):
        low = (lane // (bit * SBLK)) % 2 == 0
        for i in range(8):
            if not i & bit:
                a, b = v[i], v[i + bit]
                v[i] = jnp.where(low, a, pltpu.roll(b, bit * SBLK, 1))
                v[i + bit] = jnp.where(low, pltpu.roll(a, LANES - bit * SBLK, 1), b)
    return v


def correlate_kernel(sizes, slots_ref, left_ref, right_ref, r_ref, u_ref, v_ref, out_ref, arr, vis, blocks):
    owners, times, frames = sizes
    group2 = r_ref.shape[1]
    total = times * frames
    stations = owners * SBLK
    sides = stations // LANES
    scale = 1.0 / math.sqrt(total)

    def turn(t, _):
        for tile in range(frames // 8):
            for side in range(sides):
                got = [
                    r_ref[(side * 8 + i) * times + t, :, tile * LANES : (tile + 1) * LANES].astype(F32)
                    for i in range(8)
                ]
                for i, w in enumerate(swap_groups(got)):
                    arr[side, pl.ds(t * frames + tile * 8 + i, group2, stride=total), :] = w
        return 0

    lax.fori_loop(0, times, turn, 0)

    def correlate(g, _):
        def part(c):
            at = pl.ds(pl.multiple_of((2 * g + c) * total, total), total)
            return jnp.concatenate([arr[side, at, :] for side in range(sides)], axis=1)

        re, im = part(0), part(1)
        left = jnp.concatenate([re, im], axis=0).astype(BF)
        for c in range(2):
            right = left if c == 0 else jnp.concatenate([-im, re], axis=0).astype(BF)
            z = lax.dot_general(left, right, TN, preferred_element_type=F32) * scale
            for side in range(sides):
                vis[side, pl.ds(2 * g + c, stations, stride=group2), :] = z[
                    :, side * LANES : (side + 1) * LANES
                ]
        return 0

    lax.fori_loop(0, group2 // 2, correlate, 0)

    def regroup(p, _):
        for side in range(sides):

            @pl.when(p < side * 8 + 7)
            def _():
                for half in range(2):
                    got = [
                        vis[side, pl.ds(pl.multiple_of((p * SBLK + half * 8 + i) * group2, group2), group2), :]
                        for i in range(8)
                    ]
                    for i, w in enumerate(swap_groups(got)):
                        blocks[p * owners + side * 8 + i, :, half * LANES : (half + 1) * LANES] = w.astype(BF)

        return 0

    lax.fori_loop(0, owners - 1, regroup, 0)

    out_ref[...] = jnp.zeros_like(out_ref)
    cells = SBLK * SBLK

    def grid(m, _):
        at = pl.ds(pl.multiple_of(m * cells, cells), cells)
        u, v = u_ref[:, at].astype(F32), v_ref[:, at].astype(F32)
        kernel = jnp.concatenate([u[i : i + 1, :] * v for i in range(GRID)], axis=0).astype(BF)
        z = lax.dot_general(
            blocks[left_ref[m] * owners + right_ref[m]], kernel, NT, preferred_element_type=F32
        )
        slot = slots_ref[m]
        out_ref[slot] = out_ref[slot] + z
        return 0

    lax.fori_loop(0, owners * (owners - 1) // 2, grid, 0, unroll=2)


def correlate(turned, slots, left, right, kern_u, kern_v, owners, times, frames, tiles):
    group2 = turned.shape[1]
    stations = owners * SBLK
    whole = pl.BlockSpec(memory_space=pltpu.VMEM)
    smem = pl.BlockSpec(memory_space=pltpu.SMEM)
    return pl.pallas_call(
        functools.partial(correlate_kernel, (owners, times, frames)),
        out_shape=jax.ShapeDtypeStruct((tiles, group2, GRID * GRID), F32),
        in_specs=[smem] * 3 + [whole] * 3,
        out_specs=whole,
        scratch_shapes=[
            pltpu.VMEM((stations // LANES, group2 * times * frames, LANES), F32),
            pltpu.VMEM((stations // LANES, stations * group2, LANES), F32),
            pltpu.VMEM((owners * owners, group2, SBLK * SBLK), BF),
        ],
        compiler_params=pltpu.CompilerParams(vmem_limit_bytes=50 << 20),
        name="correlate",
    )(slots, left, right, turned, kern_u, kern_v)


def body(samples, taps, block_tile, tile_slots, kern_u, kern_v):
    frame_count = samples.shape[1]
    chan_size = lax.axis_size("chan")
    tm_size = lax.axis_size("tm")
    history = lax.ppermute(
        samples[:, frame_count - HALO :], "tm", [(i, i + 1) for i in range(tm_size - 1)]
    )
    spectra = channelize(samples, history, taps)
    turned = lax.all_to_all(spectra, ("chan", "tm"), split_axis=0, concat_axis=0, tiled=True)
    left, right = np.triu_indices(chan_size, 1)
    tile_count = tile_slots.shape[0]
    slot_ids = jnp.arange(tile_count, dtype=jnp.int32)
    slots = jnp.sum(
        jnp.where(block_tile[:, None] == tile_slots[None, :], slot_ids[None, :], 0), axis=1
    )
    grids = correlate(
        turned,
        slots,
        jnp.asarray(left, jnp.int32),
        jnp.asarray(right, jnp.int32),
        kern_u,
        kern_v,
        chan_size,
        tm_size,
        frame_count,
        tile_count,
    )
    width = grids.shape[1] // 2
    partial_value = grids.reshape(tile_count, width, 2, GRID * GRID)
    return lax.all_to_all(partial_value, "tm", split_axis=0, concat_axis=1, tiled=True)


def solution(mesh):
    placed = (P("chan", "tm", None), P(), P(), P(), P(), P())
    return jax.shard_map(
        body, mesh=mesh, in_specs=placed, out_specs=P("tm", "chan", None, None), check_vma=False
    )
```

```python
import functools
import math

import jax
import jax.numpy as jnp
import ml_dtypes
import numpy as np
from jax import lax
from jax.experimental import pallas as pl
from jax.experimental.pallas import tpu as pltpu
from jax.sharding import PartitionSpec as P

SBLK = 16
GRID = 16
RADIX = 16
HALO = 8
PITCH = 24
PAD = 8
LANES = 128
BF = jnp.bfloat16
F32 = jnp.float32
NT = (((1,), (1,)), ((), ()))
TN = (((0,), (0,)), ((), ()))


def dft_tables(length):
    span = length // RADIX
    place = np.arange(span)[None, :]
    dest = np.arange(length // (2 * RADIX))[:, None]

    def table(low):
        angle = (place * (low + RADIX * dest) % length) * (2.0 * np.pi / length)
        c, s = np.cos(angle), np.sin(angle)
        sign = -1.0 if low > RADIX // 2 else 1.0
        return np.block([[c, sign * s], [-s, sign * c]]) / math.sqrt(length)

    pairs = np.stack(
        [np.concatenate([table(k), table(RADIX - k)], axis=0) for k in range(1, RADIX // 2)]
    )
    ends = np.stack([table(0)[:, :span], table(RADIX // 2)[:, :span]])
    return pairs.astype(ml_dtypes.bfloat16), ends.astype(ml_dtypes.bfloat16)


def real_dft(x):
    n = len(x)
    if n == 2:
        return [(x[0] + x[1], None), (x[0] - x[1], None)]
    even, odd = real_dft(x[0::2]), real_dft(x[1::2])
    out = [None] * (n // 2 + 1)
    for k in range(n // 4 + 1):
        er, ei = even[k]
        dr, di = odd[k]
        if k == 0:
            out[0], out[n // 2] = (er + dr, None), (er - dr, None)
        elif k == n // 4:
            out[k] = (er, -dr)
        else:
            c, s = math.cos(2 * math.pi * k / n), math.sin(2 * math.pi * k / n)
            if 8 * k == n:
                tr, ti = (dr + di) * c, (di - dr) * c
            else:
                tr, ti = dr * c + di * s, di * c - dr * s
            out[k] = (er + tr, ei + ti)
            out[n // 2 - k] = (er - tr, ti - ei)
    return out


def channelize_kernel(
    keep_ref, x_ref, left_ref, right_ref, taps_ref, pairs_ref, ends_ref, out_ref, xs, filt, low, turned
):
    stations, frames, length = x_ref.shape
    taps = taps_ref.shape[0]
    span = length // RADIX
    rows = stations * frames
    dests = length // (2 * RADIX)
    pitch = 2 * RADIX + PAD
    own = keep_ref[0]

    for half in range(span // LANES):

        def fir(tile, _):
            at = pl.ds(pl.multiple_of(tile * span + half * LANES, LANES), LANES)
            for s in range(stations):
                for ref, first in ((left_ref, 0), (x_ref, HALO), (right_ref, HALO + frames)):
                    xs[pl.ds(first * PITCH + s, ref.shape[1], stride=PITCH), :] = ref[
                        s, :, at
                    ].astype(F32)
            weights = [taps_ref[pl.ds(k, 1), at] for k in range(taps)]
            sums = {}
            for step in range(frames + taps - 1):
                if step == HALO + frames:
                    sums = {b: own * value for b, value in sums.items()}
                x = xs[step * PITCH : step * PITCH + stations, :]
                for k in range(taps - 1, -1, -1):
                    b = step - (taps - 1) + k
                    if 0 <= b < frames:
                        term = weights[k] * x
                        sums[b] = sums[b] + term if b in sums else term
                if step >= taps - 1:
                    b = step - (taps - 1)
                    filt[tile, b * stations : (b + 1) * stations, :] = sums.pop(b).astype(BF)
            return 0

        lax.fori_loop(0, RADIX, fir, 0)

        def butterfly(b, _):
            at = pl.ds(pl.multiple_of(b * stations, stations), stations)
            parts = real_dft([filt[tile, at, :].astype(F32) for tile in range(RADIX)])
            to = slice(half * LANES, (half + 1) * LANES)
            for k, (re, im) in enumerate(parts):
                low[k, at, to] = re.astype(BF)
                if im is not None:
                    low[RADIX // 2 + k, at, to] = im.astype(BF)
            return 0

        lax.fori_loop(0, frames, butterfly, 0)

    def keep(channel, part, value):
        for tile in range(rows // LANES):
            turned[
                tile, pl.ds(channel * 2 + part, dests, stride=pitch), :
            ] = value[:, tile * LANES : (tile + 1) * LANES]

    for end in range(2):
        z = lax.dot_general(
            ends_ref[end], low[end * (RADIX // 2)], NT, preferred_element_type=F32
        )
        for part in range(2):
            keep(end * (RADIX // 2), part, z[part * dests : (part + 1) * dests])

    def pair(k, _):
        spectrum = jnp.concatenate([low[k], low[RADIX // 2 + k]], axis=1)
        for mirrored in range(2):
            z = lax.dot_general(
                pairs_ref[k - 1, mirrored * 2 * dests : (mirrored + 1) * 2 * dests, :],
                spectrum,
                NT,
                preferred_element_type=F32,
            )
            channel = RADIX - k if mirrored else k
            for part in range(2):
                keep(channel, part, z[part * dests : (part + 1) * dests])
        return 0

    lax.fori_loop(1, RADIX // 2, pair, 0)

    def give(d, _):
        at = pl.ds(pl.multiple_of(d * pitch, 8), 2 * RADIX)
        for tile in range(rows // LANES):
            out_ref[d, :, tile * LANES : (tile + 1) * LANES] = turned[tile, at, :].astype(BF)
        return 0

    lax.fori_loop(0, dests, give, 0, unroll=4)


def channelize(keep, samples, before, after, taps):
    stations, frames, length = samples.shape
    rows = stations * frames
    span = length // RADIX
    dests = length // (2 * RADIX)
    pairs, ends = dft_tables(length)
    whole = pl.BlockSpec(memory_space=pltpu.VMEM)
    return pl.pallas_call(
        channelize_kernel,
        out_shape=jax.ShapeDtypeStruct((dests, 2 * RADIX, rows), BF),
        in_specs=[pl.BlockSpec(memory_space=pltpu.SMEM)] + [whole] * 6,
        out_specs=whole,
        scratch_shapes=[
            pltpu.VMEM(((2 * HALO + frames) * PITCH, LANES), F32),
            pltpu.VMEM((RADIX, rows, LANES), BF),
            pltpu.VMEM((RADIX, rows, span), BF),
            pltpu.VMEM((rows // LANES, dests * (2 * RADIX + PAD), LANES), F32),
        ],
        compiler_params=pltpu.CompilerParams(vmem_limit_bytes=50 << 20),
        name="channelize",
    )(keep, samples, before, after, taps, jnp.asarray(pairs), jnp.asarray(ends))


def swap_groups(v):
    lane = lax.broadcasted_iota(jnp.int32, v[0].shape, 1)
    v = list(v)
    for bit in (1, 2, 4):
        low = (lane // (bit * SBLK)) % 2 == 0
        for i in range(8):
            if not i & bit:
                a, b = v[i], v[i + bit]
                v[i] = jnp.where(low, a, pltpu.roll(b, bit * SBLK, 1))
                v[i + bit] = jnp.where(low, pltpu.roll(a, LANES - bit * SBLK, 1), b)
    return v


def weights_kernel(u_ref, v_ref, out_ref):
    cells = SBLK * SBLK
    for m in range(out_ref.shape[0]):
        u = u_ref[:, m * cells : (m + 1) * cells].astype(F32)
        v = v_ref[:, m * cells : (m + 1) * cells].astype(F32)
        for i in range(GRID):
            out_ref[m, i * GRID : (i + 1) * GRID, :] = (u[i : i + 1, :] * v).astype(BF)


def grid_weights(kern_u, kern_v):
    cells = SBLK * SBLK
    count = kern_u.shape[1] // cells
    step = math.gcd(count, 8)
    part = pl.BlockSpec((GRID, step * cells), lambda m: (0, m))
    return pl.pallas_call(
        weights_kernel,
        grid=(count // step,),
        out_shape=jax.ShapeDtypeStruct((count, GRID * GRID, cells), BF),
        in_specs=[part, part],
        out_specs=pl.BlockSpec((step, GRID * GRID, cells), lambda m: (m, 0, 0)),
        compiler_params=pltpu.CompilerParams(vmem_limit_bytes=16 << 20),
        cost_estimate=pl.CostEstimate(
            flops=count * GRID * GRID * cells, bytes_accessed=2 * count * GRID * GRID * cells, transcendentals=0
        ),
        name="grid_weights",
    )(kern_u, kern_v)


def correlate_kernel(sizes, slots_ref, pair_ref, r_ref, k_ref, out_ref, arr, vis, blocks, weights, acc, sem):
    owners, times, frames = sizes
    group2 = r_ref.shape[1]
    total = times * frames
    stations = owners * SBLK
    sides = stations // LANES
    arr_pitch = total + PAD
    vis_pitch = group2 + PAD
    fetch = pltpu.make_async_copy(k_ref, weights, sem)
    fetch.start()

    def turn(t, _):
        for tile in range(frames // 8):
            for side in range(sides):
                got = [
                    r_ref[(side * 8 + i) * times + t, :, tile * LANES : (tile + 1) * LANES]
                    for i in range(8)
                ]
                for i, w in enumerate(swap_groups(got)):
                    arr[side, pl.ds(t * frames + tile * 8 + i, group2, stride=arr_pitch), :] = w.astype(F32)
        return 0

    lax.fori_loop(0, times, turn, 0)

    def correlate(g, _):
        def part(side, c):
            at = pl.ds(pl.multiple_of((2 * g + c) * arr_pitch, 8), total)
            return arr[side, at, :].astype(BF)

        re = [part(side, 0) for side in range(sides)]
        im = [part(side, 1) for side in range(sides)]
        for side in range(sides):
            left = jnp.concatenate(
                [jnp.concatenate(re[: side + 1], axis=1), jnp.concatenate(im[: side + 1], axis=1)], axis=0
            )
            right = jnp.concatenate(
                [
                    jnp.concatenate([re[side], -im[side]], axis=1),
                    jnp.concatenate([im[side], re[side]], axis=1),
                ],
                axis=0,
            )
            z = lax.dot_general(left, right, TN, preferred_element_type=F32)
            for c in range(2):
                vis[side, pl.ds(2 * g + c, (side + 1) * LANES, stride=vis_pitch), :] = z[
                    :, c * LANES : (c + 1) * LANES
                ]
        return 0

    lax.fori_loop(0, group2 // 2, correlate, 0)

    def regroup(p, _):
        for side in range(sides):

            @pl.when(p < side * 8 + 7)
            def _():
                for half in range(2):
                    got = [
                        vis[
                            side,
                            pl.ds(pl.multiple_of((p * SBLK + half * 8 + i) * vis_pitch, 8), group2),
                            :,
                        ].astype(BF)
                        for i in range(8)
                    ]
                    for i, w in enumerate(swap_groups(got)):
                        blocks[p * owners + side * 8 + i, :, half * LANES : (half + 1) * LANES] = w

        return 0

    lax.fori_loop(0, owners - 1, regroup, 0)

    acc[...] = jnp.zeros_like(acc)
    fetch.wait()

    def grid(m, _):
        z = lax.dot_general(blocks[pair_ref[m]], weights[m], NT, preferred_element_type=F32)
        slot = slots_ref[m]
        acc[slot] = acc[slot] + z
        return 0

    lax.fori_loop(0, owners * (owners - 1) // 2, grid, 0, unroll=4)
    out_ref[...] = (acc[...] * (1.0 / math.sqrt(total))).astype(BF)


def correlate(turned, slots, pair, weights, owners, times, frames, tiles):
    group2 = turned.shape[1]
    stations = owners * SBLK
    whole = pl.BlockSpec(memory_space=pltpu.VMEM)
    smem = pl.BlockSpec(memory_space=pltpu.SMEM)
    return pl.pallas_call(
        functools.partial(correlate_kernel, (owners, times, frames)),
        out_shape=jax.ShapeDtypeStruct((tiles, group2, GRID * GRID), BF),
        in_specs=[smem, smem, whole, pl.BlockSpec(memory_space=pl.ANY)],
        out_specs=whole,
        scratch_shapes=[
            pltpu.VMEM((stations // LANES, group2 * (times * frames + PAD), LANES), F32),
            pltpu.VMEM((stations // LANES, stations * (group2 + PAD), LANES), F32),
            pltpu.VMEM((owners * owners, group2, SBLK * SBLK), BF),
            pltpu.VMEM(weights.shape, BF),
            pltpu.VMEM((tiles, group2, GRID * GRID), F32),
            pltpu.SemaphoreType.DMA,
        ],
        compiler_params=pltpu.CompilerParams(vmem_limit_bytes=52 << 20),
        name="correlate",
    )(slots, pair, turned, weights)


def body(samples, taps, block_tile, tile_slots, kern_u, kern_v):
    frame_count = samples.shape[1]
    chan_size = lax.axis_size("chan")
    tm_size = lax.axis_size("tm")
    before = lax.ppermute(
        samples[:, frame_count - HALO :], "tm", [(i, i + 1) for i in range(tm_size - 1)]
    )
    after = lax.ppermute(
        samples[:, :HALO], "tm", [((i + 1) % tm_size, i) for i in range(tm_size)]
    )
    keep = (lax.axis_index("tm") < tm_size - 1).astype(F32).reshape(1)
    weights = grid_weights(kern_u, kern_v)
    spectra = channelize(keep, samples, before, after, taps)
    turned = lax.all_to_all(spectra, ("chan", "tm"), split_axis=0, concat_axis=0, tiled=True)
    left, right = np.triu_indices(chan_size, 1)
    tile_count = tile_slots.shape[0]
    slot_ids = jnp.arange(tile_count, dtype=jnp.int32)
    slots = jnp.sum(
        jnp.where(block_tile[:, None] == tile_slots[None, :], slot_ids[None, :], 0), axis=1
    )
    pair = jnp.asarray(left * chan_size + right, jnp.int32)
    grids = correlate(turned, slots, pair, weights, chan_size, tm_size, frame_count, tile_count)
    width = grids.shape[1] // 2
    partial_value = grids.reshape(tile_count, width, 2, GRID * GRID)
    return lax.all_to_all(partial_value, "tm", split_axis=0, concat_axis=1, tiled=True).astype(F32)


def solution(mesh):
    placed = (P("chan", "tm", None), P(), P(), P(), P(), P())
    return jax.shard_map(
        body, mesh=mesh, in_specs=placed, out_specs=P("tm", "chan", None, None), check_vma=False
    )
```

```python
import functools
import math

import jax
import jax.numpy as jnp
import ml_dtypes
import numpy as np
from jax import lax
from jax.experimental import pallas as pl
from jax.experimental.pallas import tpu as pltpu
from jax.sharding import PartitionSpec as P

SBLK = 16
GRID = 16
RADIX = 16
HALO = 8
PITCH = 24
PAD = 8
LANES = 128
BF = jnp.bfloat16
F32 = jnp.float32
NT = (((1,), (1,)), ((), ()))
TN = (((0,), (0,)), ((), ()))


def dft_tables(length):
    span = length // RADIX
    place = np.arange(span)[None, :]
    dest = np.arange(length // (2 * RADIX))[:, None]

    def table(low):
        angle = (place * (low + RADIX * dest) % length) * (2.0 * np.pi / length)
        c, s = np.cos(angle), np.sin(angle)
        sign = -1.0 if low > RADIX // 2 else 1.0
        return np.block([[c, sign * s], [-s, sign * c]]) / math.sqrt(length)

    pairs = np.stack(
        [np.concatenate([table(k), table(RADIX - k)], axis=0) for k in range(1, RADIX // 2)]
    )
    ends = np.stack([table(0)[:, :span], table(RADIX // 2)[:, :span]])
    return pairs.astype(ml_dtypes.bfloat16), ends.astype(ml_dtypes.bfloat16)


def real_dft(x):
    n = len(x)
    if n == 2:
        return [(x[0] + x[1], None), (x[0] - x[1], None)]
    even, odd = real_dft(x[0::2]), real_dft(x[1::2])
    out = [None] * (n // 2 + 1)
    for k in range(n // 4 + 1):
        er, ei = even[k]
        dr, di = odd[k]
        if k == 0:
            out[0], out[n // 2] = (er + dr, None), (er - dr, None)
        elif k == n // 4:
            out[k] = (er, -dr)
        else:
            c, s = math.cos(2 * math.pi * k / n), math.sin(2 * math.pi * k / n)
            if 8 * k == n:
                tr, ti = (dr + di) * c, (di - dr) * c
            else:
                tr, ti = dr * c + di * s, di * c - dr * s
            out[k] = (er + tr, ei + ti)
            out[n // 2 - k] = (er - tr, ti - ei)
    return out


def spread(source, target, first, at):
    for s in range(source.shape[0]):
        target[pl.ds(first * PITCH + s, source.shape[1], stride=PITCH), :] = source[s, :, at].astype(F32)


def butterflies(filt, low, half):
    to = slice(half * LANES, (half + 1) * LANES)

    def butterfly(b, _):
        at = pl.ds(pl.multiple_of(b * SBLK, SBLK), SBLK)
        parts = real_dft([filt[tile, at, :].astype(F32) for tile in range(RADIX)])
        for k, (re, im) in enumerate(parts):
            low[k, at, to] = re.astype(BF)
            if im is not None:
                low[RADIX // 2 + k, at, to] = im.astype(BF)
        return 0

    lax.fori_loop(0, filt.shape[1] // SBLK, butterfly, 0, unroll=2)


def products(low, turned, pairs_ref, ends_ref):
    dests = ends_ref.shape[1] // 2
    pitch = 2 * RADIX + PAD

    def keep(channel, part, value):
        for tile in range(low.shape[1] // LANES):
            turned[tile, pl.ds(channel * 2 + part, dests, stride=pitch), :] = value[
                :, tile * LANES : (tile + 1) * LANES
            ]

    for end in range(2):
        z = lax.dot_general(
            ends_ref[end], low[end * (RADIX // 2)], NT, preferred_element_type=F32
        )
        for part in range(2):
            keep(end * (RADIX // 2), part, z[part * dests : (part + 1) * dests])

    def pair(k, _):
        spectrum = jnp.concatenate([low[k], low[RADIX // 2 + k]], axis=1)
        for mirrored in range(2):
            z = lax.dot_general(
                pairs_ref[k - 1, mirrored * 2 * dests : (mirrored + 1) * 2 * dests, :],
                spectrum,
                NT,
                preferred_element_type=F32,
            )
            channel = RADIX - k if mirrored else k
            for part in range(2):
                keep(channel, part, z[part * dests : (part + 1) * dests])
        return 0

    lax.fori_loop(1, RADIX // 2, pair, 0)


def own_kernel(keep_ref, x_ref, taps_ref, pairs_ref, ends_ref, out_ref, part_ref, xs, filt, low, turned):
    stations, frames, length = x_ref.shape
    taps = taps_ref.shape[0]
    span = length // RADIX
    own = keep_ref[0]
    done = range(HALO, 2 * HALO)

    for half in range(span // LANES):

        def fir(tile, _):
            at = pl.ds(pl.multiple_of(tile * span + half * LANES, LANES), LANES)
            spread(x_ref, xs, 0, at)
            weights = [taps_ref[pl.ds(k, 1), at] for k in range(taps)]
            sums = {}
            for step in range(frames):
                x = xs[step * PITCH : step * PITCH + stations, :]
                for k in range(taps - 1, -1, -1):
                    b = step + HALO - (taps - 1) + k
                    if 0 <= b < frames:
                        term = weights[k] * x
                        sums[b] = sums[b] + term if b in sums else term
                ready = [b for b in sums if b == step + HALO - (taps - 1) or step == frames - 1]
                for b in ready:
                    value = sums.pop(b)
                    if b in done:
                        place = b - done.start
                        filt[tile, place * stations : (place + 1) * stations, :] = value.astype(BF)
                    else:
                        place = b if b < done.start else b - len(done)
                        if b + taps - 1 >= HALO + frames:
                            value = own * value
                        part_ref[2 * tile + half, place * stations : (place + 1) * stations, :] = value
            return 0

        lax.fori_loop(0, RADIX, fir, 0)
        butterflies(filt, low, half)

    products(low, turned, pairs_ref, ends_ref)

    def give(d, _):
        at = pl.ds(pl.multiple_of(d * (2 * RADIX + PAD), 8), 2 * RADIX)
        out_ref[d] = turned[0, at, :].astype(BF)
        return 0

    lax.fori_loop(0, out_ref.shape[0], give, 0, unroll=8)


def rest_kernel(left_ref, right_ref, taps_ref, pairs_ref, ends_ref, done_ref, part_ref, out_ref, xs, filt, low, turned):
    stations, _, length = left_ref.shape
    taps = taps_ref.shape[0]
    span = length // RADIX
    count = part_ref.shape[1] // stations

    for half in range(span // LANES):

        def fir(tile, _):
            at = pl.ds(pl.multiple_of(tile * span + half * LANES, LANES), LANES)
            spread(left_ref, xs, 0, at)
            spread(right_ref, xs, HALO, at)
            weights = [taps_ref[pl.ds(k, 1), at] for k in range(taps)]
            x = [xs[step * PITCH : step * PITCH + stations, :] for step in range(2 * HALO)]
            for place in range(count):
                to = slice(place * stations, (place + 1) * stations)
                value = part_ref[2 * tile + half, to, :]
                if place < HALO:
                    terms = [(j, taps - 1 - (j - place)) for j in range(place, HALO)]
                else:
                    first = place - (count - (HALO - 1))
                    terms = [(HALO + j, first - j) for j in range(first + 1)]
                for j, k in terms:
                    value = value + weights[k] * x[j]
                filt[tile, to, :] = value.astype(BF)
            return 0

        lax.fori_loop(0, RADIX, fir, 0)
        butterflies(filt, low, half)

    products(low, turned, pairs_ref, ends_ref)
    tiles = low.shape[1] // LANES

    def give(d, _):
        at = pl.ds(pl.multiple_of(d * (2 * RADIX + PAD), 8), 2 * RADIX)
        for tile in range(tiles):
            out_ref[d, :, tile * LANES : (tile + 1) * LANES] = turned[tile, at, :].astype(BF)
        out_ref[d, :, tiles * LANES :] = done_ref[d]
        return 0

    lax.fori_loop(0, out_ref.shape[0], give, 0, unroll=8)


def channel_scratch(frames, steps, length):
    rows = frames * SBLK
    return [
        pltpu.VMEM((steps * PITCH, LANES), F32),
        pltpu.VMEM((RADIX, rows, LANES), BF),
        pltpu.VMEM((RADIX, rows, length // RADIX), BF),
        pltpu.VMEM((rows // LANES, length // (2 * RADIX) * (2 * RADIX + PAD), LANES), F32),
    ]


def channelize_own(keep, samples, taps, pairs, ends):
    stations, frames, length = samples.shape
    dests = length // (2 * RADIX)
    whole = pl.BlockSpec(memory_space=pltpu.VMEM)
    return pl.pallas_call(
        own_kernel,
        out_shape=[
            jax.ShapeDtypeStruct((dests, 2 * RADIX, HALO * stations), BF),
            jax.ShapeDtypeStruct((length // LANES, (frames - HALO) * stations, LANES), F32),
        ],
        in_specs=[pl.BlockSpec(memory_space=pltpu.SMEM)] + [whole] * 4,
        out_specs=[whole] * 2,
        scratch_shapes=channel_scratch(HALO, frames, length),
        compiler_params=pltpu.CompilerParams(vmem_limit_bytes=32 << 20),
        cost_estimate=pl.CostEstimate(
            flops=10 * samples.size * 1000, bytes_accessed=20 << 20, transcendentals=0
        ),
        name="own",
    )(keep, samples, taps, pairs, ends)


def channelize_rest(before, after, taps, pairs, ends, done, part):
    stations, _, length = before.shape
    dests = length // (2 * RADIX)
    frames = part.shape[1] // stations
    whole = pl.BlockSpec(memory_space=pltpu.VMEM)
    return pl.pallas_call(
        rest_kernel,
        out_shape=jax.ShapeDtypeStruct((dests, 2 * RADIX, part.shape[1] + done.shape[2]), BF),
        in_specs=[whole] * 7,
        out_specs=whole,
        scratch_shapes=channel_scratch(frames, 2 * HALO, length),
        compiler_params=pltpu.CompilerParams(vmem_limit_bytes=32 << 20),
        name="rest",
    )(before, after, taps, pairs, ends, done, part)


def swap_groups(v):
    lane = lax.broadcasted_iota(jnp.int32, v[0].shape, 1)
    v = list(v)
    for bit in (1, 2, 4):
        low = (lane // (bit * SBLK)) % 2 == 0
        for i in range(8):
            if not i & bit:
                a, b = v[i], v[i + bit]
                v[i] = jnp.where(low, a, pltpu.roll(b, bit * SBLK, 1))
                v[i + bit] = jnp.where(low, pltpu.roll(a, LANES - bit * SBLK, 1), b)
    return v


def weights_kernel(u_ref, v_ref, out_ref):
    cells = SBLK * SBLK
    for m in range(out_ref.shape[0]):
        u = u_ref[:, m * cells : (m + 1) * cells].astype(F32)
        v = v_ref[:, m * cells : (m + 1) * cells].astype(F32)
        cell_rows = jnp.concatenate([u[i : i + 1, :] * v for i in range(GRID)], axis=0)
        out_ref[m] = cell_rows.T.astype(BF)


def grid_weights(kern_u, kern_v):
    cells = SBLK * SBLK
    count = kern_u.shape[1] // cells
    step = math.gcd(count, 8)
    part = pl.BlockSpec((GRID, step * cells), lambda m: (0, m))
    return pl.pallas_call(
        weights_kernel,
        grid=(count // step,),
        out_shape=jax.ShapeDtypeStruct((count, cells, GRID * GRID), BF),
        in_specs=[part, part],
        out_specs=pl.BlockSpec((step, cells, GRID * GRID), lambda m: (m, 0, 0)),
        compiler_params=pltpu.CompilerParams(vmem_limit_bytes=16 << 20),
        cost_estimate=pl.CostEstimate(
            flops=count * GRID * GRID * cells, bytes_accessed=2 * count * GRID * GRID * cells, transcendentals=0
        ),
        name="grid_weights",
    )(kern_u, kern_v)


def correlate_kernel(sizes, slots_ref, r_ref, k_ref, out_ref, arr, vis, weights, acc, sem):
    owners, times, frames = sizes
    group2 = r_ref.shape[1]
    total = times * frames
    stations = owners * SBLK
    sides = stations // LANES
    arr_pitch = total + PAD
    vis_pitch = group2 + PAD
    fetch = pltpu.make_async_copy(k_ref, weights, sem)
    fetch.start()

    def turn(t, _):
        for tile in range(frames // 8):
            for side in range(sides):
                got = [
                    r_ref[(side * 8 + i) * times + t, :, tile * LANES : (tile + 1) * LANES]
                    for i in range(8)
                ]
                for i, w in enumerate(swap_groups(got)):
                    arr[side, pl.ds(t * frames + tile * 8 + i, group2, stride=arr_pitch), :] = w.astype(F32)
        return 0

    lax.fori_loop(0, times, turn, 0)

    def correlate(g, _):
        def part(side, c):
            at = pl.ds(pl.multiple_of((2 * g + c) * arr_pitch, 8), total)
            return arr[side, at, :].astype(BF)

        re = [part(side, 0) for side in range(sides)]
        im = [part(side, 1) for side in range(sides)]
        for side in range(sides):
            left = jnp.concatenate(
                [jnp.concatenate(re[: side + 1], axis=1), jnp.concatenate(im[: side + 1], axis=1)], axis=0
            )
            right = jnp.concatenate(
                [
                    jnp.concatenate([re[side], -im[side]], axis=1),
                    jnp.concatenate([im[side], re[side]], axis=1),
                ],
                axis=0,
            )
            z = lax.dot_general(left, right, TN, preferred_element_type=F32)
            for c in range(2):
                vis[side, pl.ds(2 * g + c, (side + 1) * LANES, stride=vis_pitch), :] = z[
                    :, c * LANES : (c + 1) * LANES
                ]
        return 0

    lax.fori_loop(0, group2 // 2, correlate, 0, unroll=2)

    acc[...] = jnp.zeros_like(acc)
    fetch.wait()

    m = 0
    for p in range(owners - 1):
        halves = {}
        for side in range(sides):
            if p >= side * 8 + 7:
                continue
            for half in range(2):
                got = [
                    vis[side, pl.ds((p * SBLK + half * 8 + i) * vis_pitch, group2), :].astype(BF)
                    for i in range(8)
                ]
                for i, w in enumerate(swap_groups(got)):
                    halves[side * 8 + i, half] = w
        for q in range(p + 1, owners):
            block = jnp.concatenate([halves[q, 0], halves[q, 1]], axis=1)
            z = jnp.dot(block, weights[m], preferred_element_type=F32)
            slot = slots_ref[m]
            acc[slot] = acc[slot] + z
            m += 1
    out_ref[...] = (acc[...] * (1.0 / math.sqrt(total))).astype(BF)


def correlate(turned, slots, weights, owners, times, frames, tiles):
    group2 = turned.shape[1]
    stations = owners * SBLK
    whole = pl.BlockSpec(memory_space=pltpu.VMEM)
    smem = pl.BlockSpec(memory_space=pltpu.SMEM)
    return pl.pallas_call(
        functools.partial(correlate_kernel, (owners, times, frames)),
        out_shape=jax.ShapeDtypeStruct((tiles, group2, GRID * GRID), BF),
        in_specs=[smem, whole, pl.BlockSpec(memory_space=pl.ANY)],
        out_specs=whole,
        scratch_shapes=[
            pltpu.VMEM((stations // LANES, group2 * (times * frames + PAD), LANES), F32),
            pltpu.VMEM((stations // LANES, stations * (group2 + PAD), LANES), F32),
            pltpu.VMEM(weights.shape, BF),
            pltpu.VMEM((tiles, group2, GRID * GRID), F32),
            pltpu.SemaphoreType.DMA,
        ],
        compiler_params=pltpu.CompilerParams(vmem_limit_bytes=42 << 20),
        name="correlate",
    )(slots, turned, weights)


def body(samples, taps, block_tile, tile_slots, kern_u, kern_v):
    frame_count = samples.shape[1]
    chan_size = lax.axis_size("chan")
    tm_size = lax.axis_size("tm")
    before = lax.ppermute(
        samples[:, frame_count - HALO :], "tm", [(i, i + 1) for i in range(tm_size - 1)]
    )
    after = lax.ppermute(
        samples[:, :HALO], "tm", [((i + 1) % tm_size, i) for i in range(tm_size)]
    )
    keep = (lax.axis_index("tm") < tm_size - 1).astype(F32).reshape(1)
    weights = grid_weights(kern_u, kern_v)
    pairs, ends = (jnp.asarray(table) for table in dft_tables(samples.shape[2]))
    done, part = channelize_own(keep, samples, taps, pairs, ends)
    spectra = channelize_rest(before, after, taps, pairs, ends, done, part)
    turned = lax.all_to_all(spectra, ("chan", "tm"), split_axis=0, concat_axis=0, tiled=True)
    tile_count = tile_slots.shape[0]
    slot_ids = jnp.arange(tile_count, dtype=jnp.int32)
    slots = jnp.sum(
        jnp.where(block_tile[:, None] == tile_slots[None, :], slot_ids[None, :], 0), axis=1
    )
    grids = correlate(turned, slots, weights, chan_size, tm_size, frame_count, tile_count)
    width = grids.shape[1] // 2
    partial_value = grids.reshape(tile_count, width, 2, GRID * GRID)
    return lax.all_to_all(partial_value, "tm", split_axis=0, concat_axis=1, tiled=True).astype(F32)


def solution(mesh):
    placed = (P("chan", "tm", None), P(), P(), P(), P(), P())
    return jax.shard_map(
        body, mesh=mesh, in_specs=placed, out_specs=P("tm", "chan", None, None), check_vma=False
    )
```

```python
import functools
import math

import jax
import jax.numpy as jnp
import ml_dtypes
import numpy as np
from jax import lax
from jax.experimental import pallas as pl
from jax.experimental.pallas import tpu as pltpu
from jax.sharding import PartitionSpec as P

SBLK = 16
GRID = 16
RADIX = 16
HALO = 8
PITCH = 24
PAD = 8
LANES = 128
BF = jnp.bfloat16
F32 = jnp.float32
NT = (((1,), (1,)), ((), ()))
TN = (((0,), (0,)), ((), ()))


def dft_tables(length):
    span = length // RADIX
    place = np.arange(span)[None, :]
    dest = np.arange(length // (2 * RADIX))[:, None]

    def table(low):
        angle = (place * (low + RADIX * dest) % length) * (2.0 * np.pi / length)
        c, s = np.cos(angle), np.sin(angle)
        sign = -1.0 if low > RADIX // 2 else 1.0
        return np.block([[c, sign * s], [-s, sign * c]]) / math.sqrt(length)

    pairs = np.stack(
        [np.concatenate([table(k), table(RADIX - k)], axis=0) for k in range(1, RADIX // 2)]
    )
    ends = np.stack([table(0)[:, :span], table(RADIX // 2)[:, :span]])
    return pairs.astype(ml_dtypes.bfloat16), ends.astype(ml_dtypes.bfloat16)


def real_dft(x):
    n = len(x)
    if n == 2:
        return [(x[0] + x[1], None), (x[0] - x[1], None)]
    even, odd = real_dft(x[0::2]), real_dft(x[1::2])
    out = [None] * (n // 2 + 1)
    for k in range(n // 4 + 1):
        er, ei = even[k]
        dr, di = odd[k]
        if k == 0:
            out[0], out[n // 2] = (er + dr, None), (er - dr, None)
        elif k == n // 4:
            out[k] = (er, -dr)
        else:
            c, s = math.cos(2 * math.pi * k / n), math.sin(2 * math.pi * k / n)
            if 8 * k == n:
                tr, ti = (dr + di) * c, (di - dr) * c
            else:
                tr, ti = dr * c + di * s, di * c - dr * s
            out[k] = (er + tr, ei + ti)
            out[n // 2 - k] = (er - tr, ti - ei)
    return out


def spread(source, target, first, at):
    for s in range(source.shape[0]):
        target[pl.ds(first * PITCH + s, source.shape[1], stride=PITCH), :] = source[s, :, at].astype(F32)


def butterflies(filt, low, half):
    to = slice(half * LANES, (half + 1) * LANES)

    def butterfly(b, _):
        at = pl.ds(pl.multiple_of(b * SBLK, SBLK), SBLK)
        parts = real_dft([filt[tile, at, :].astype(F32) for tile in range(RADIX)])
        for k, (re, im) in enumerate(parts):
            low[k, at, to] = re.astype(BF)
            if im is not None:
                low[RADIX // 2 + k, at, to] = im.astype(BF)
        return 0

    lax.fori_loop(0, filt.shape[1] // SBLK, butterfly, 0, unroll=2)


def products(low, turned, pairs_ref, ends_ref):
    dests = ends_ref.shape[1] // 2
    pitch = 2 * RADIX + PAD

    def keep(channel, part, value):
        for tile in range(low.shape[1] // LANES):
            turned[tile, pl.ds(channel * 2 + part, dests, stride=pitch), :] = value[
                :, tile * LANES : (tile + 1) * LANES
            ]

    for end in range(2):
        z = lax.dot_general(
            ends_ref[end], low[end * (RADIX // 2)], NT, preferred_element_type=F32
        )
        for part in range(2):
            keep(end * (RADIX // 2), part, z[part * dests : (part + 1) * dests])

    def pair(k, _):
        spectrum = jnp.concatenate([low[k], low[RADIX // 2 + k]], axis=1)
        for mirrored in range(2):
            z = lax.dot_general(
                pairs_ref[k - 1, mirrored * 2 * dests : (mirrored + 1) * 2 * dests, :],
                spectrum,
                NT,
                preferred_element_type=F32,
            )
            channel = RADIX - k if mirrored else k
            for part in range(2):
                keep(channel, part, z[part * dests : (part + 1) * dests])
        return 0

    lax.fori_loop(1, RADIX // 2, pair, 0, unroll=RADIX // 2 - 1)


def own_kernel(
    keep_ref, x_ref, taps_ref, pairs_hbm, ends_hbm, out_ref, part_ref, xs, filt, low, turned, pairs_ref, ends_ref, sems
):
    fetches = [
        pltpu.make_async_copy(pairs_hbm, pairs_ref, sems.at[0]),
        pltpu.make_async_copy(ends_hbm, ends_ref, sems.at[1]),
    ]
    for fetch in fetches:
        fetch.start()
    stations, frames, length = x_ref.shape
    taps = taps_ref.shape[0]
    span = length // RADIX
    own = keep_ref[0]
    done = range(HALO, 2 * HALO)

    for half in range(span // LANES):

        def fir(tile, _):
            at = pl.ds(pl.multiple_of(tile * span + half * LANES, LANES), LANES)
            spread(x_ref, xs, 0, at)
            weights = [taps_ref[pl.ds(k, 1), at] for k in range(taps)]
            sums = {}
            for step in range(frames):
                x = xs[step * PITCH : step * PITCH + stations, :]
                for k in range(taps - 1, -1, -1):
                    b = step + HALO - (taps - 1) + k
                    if 0 <= b < frames:
                        term = weights[k] * x
                        sums[b] = sums[b] + term if b in sums else term
                ready = [b for b in sums if b == step + HALO - (taps - 1) or step == frames - 1]
                for b in ready:
                    value = sums.pop(b)
                    if b in done:
                        place = b - done.start
                        filt[tile, place * stations : (place + 1) * stations, :] = value.astype(BF)
                    else:
                        place = b if b < done.start else b - len(done)
                        if b + taps - 1 >= HALO + frames:
                            value = own * value
                        part_ref[2 * tile + half, place * stations : (place + 1) * stations, :] = value
            return 0

        lax.fori_loop(0, RADIX, fir, 0)
        butterflies(filt, low, half)

    for fetch in fetches:
        fetch.wait()
    products(low, turned, pairs_ref, ends_ref)

    def give(d, _):
        at = pl.ds(pl.multiple_of(d * (2 * RADIX + PAD), 8), 2 * RADIX)
        out_ref[d] = turned[0, at, :].astype(BF)
        return 0

    lax.fori_loop(0, out_ref.shape[0], give, 0, unroll=8)


def rest_kernel(left_ref, right_ref, taps_ref, pairs_ref, ends_ref, done_ref, part_ref, out_ref, xs, filt, low, turned):
    stations, _, length = left_ref.shape
    taps = taps_ref.shape[0]
    span = length // RADIX
    count = part_ref.shape[1] // stations

    for half in range(span // LANES):

        def fir(tile, _):
            at = pl.ds(pl.multiple_of(tile * span + half * LANES, LANES), LANES)
            spread(left_ref, xs, 0, at)
            spread(right_ref, xs, HALO, at)
            weights = [taps_ref[pl.ds(k, 1), at] for k in range(taps)]
            x = [xs[step * PITCH : step * PITCH + stations, :] for step in range(2 * HALO)]
            for place in range(count):
                to = slice(place * stations, (place + 1) * stations)
                value = part_ref[2 * tile + half, to, :]
                if place < HALO:
                    terms = [(j, taps - 1 - (j - place)) for j in range(place, HALO)]
                else:
                    first = place - (count - (HALO - 1))
                    terms = [(HALO + j, first - j) for j in range(first + 1)]
                for j, k in terms:
                    value = value + weights[k] * x[j]
                filt[tile, to, :] = value.astype(BF)
            return 0

        lax.fori_loop(0, RADIX, fir, 0)
        butterflies(filt, low, half)

    products(low, turned, pairs_ref, ends_ref)
    tiles = low.shape[1] // LANES

    def give(d, _):
        at = pl.ds(pl.multiple_of(d * (2 * RADIX + PAD), 8), 2 * RADIX)
        for tile in range(tiles):
            out_ref[d, :, tile * LANES : (tile + 1) * LANES] = turned[tile, at, :].astype(BF)
        out_ref[d, :, tiles * LANES :] = done_ref[d]
        return 0

    lax.fori_loop(0, out_ref.shape[0], give, 0, unroll=8)


def channel_scratch(frames, steps, length):
    rows = frames * SBLK
    return [
        pltpu.VMEM((steps * PITCH, LANES), F32),
        pltpu.VMEM((RADIX, rows, LANES), BF),
        pltpu.VMEM((RADIX, rows, length // RADIX), BF),
        pltpu.VMEM((rows // LANES, length // (2 * RADIX) * (2 * RADIX + PAD), LANES), F32),
    ]


def channelize_own(keep, samples, taps, pairs, ends):
    stations, frames, length = samples.shape
    dests = length // (2 * RADIX)
    whole = pl.BlockSpec(memory_space=pltpu.VMEM)
    return pl.pallas_call(
        own_kernel,
        out_shape=[
            jax.ShapeDtypeStruct((dests, 2 * RADIX, HALO * stations), BF),
            jax.ShapeDtypeStruct((length // LANES, (frames - HALO) * stations, LANES), F32),
        ],
        in_specs=[pl.BlockSpec(memory_space=pltpu.SMEM)]
        + [whole] * 2
        + [pl.BlockSpec(memory_space=pltpu.HBM)] * 2,
        out_specs=[whole] * 2,
        scratch_shapes=channel_scratch(HALO, frames, length)
        + [
            pltpu.VMEM(pairs.shape, BF),
            pltpu.VMEM(ends.shape, BF),
            pltpu.SemaphoreType.DMA((2,)),
        ],
        compiler_params=pltpu.CompilerParams(vmem_limit_bytes=22 << 20),
        cost_estimate=pl.CostEstimate(
            flops=10 * samples.size * 1000, bytes_accessed=20 << 20, transcendentals=0
        ),
        name="own",
    )(
        keep,
        samples,
        taps,
        pltpu.with_memory_space_constraint(pairs, pltpu.HBM),
        pltpu.with_memory_space_constraint(ends, pltpu.HBM),
    )


def channelize_rest(before, after, taps, pairs, ends, done, part):
    stations, _, length = before.shape
    dests = length // (2 * RADIX)
    frames = part.shape[1] // stations
    whole = pl.BlockSpec(memory_space=pltpu.VMEM)
    return pl.pallas_call(
        rest_kernel,
        out_shape=jax.ShapeDtypeStruct((dests, 2 * RADIX, part.shape[1] + done.shape[2]), BF),
        in_specs=[whole] * 7,
        out_specs=whole,
        scratch_shapes=channel_scratch(frames, 2 * HALO, length),
        compiler_params=pltpu.CompilerParams(vmem_limit_bytes=28 << 20),
        name="rest",
    )(before, after, taps, pairs, ends, done, part)


def swap_groups(v):
    group = lax.broadcasted_iota(jnp.int32, v[0].shape, 1) // SBLK
    v = [pltpu.roll(a, i * SBLK, 1) if i else a for i, a in enumerate(v)]
    v = [v[-i % 8] for i in range(8)]
    for bit in (1, 2, 4):
        odd = (group & bit) != 0
        v = [jnp.where(odd, v[(i - bit) % 8], v[i]) for i in range(8)]
    return [pltpu.roll(a, LANES - j * SBLK, 1) if j else a for j, a in enumerate(v)]


def weights_kernel(u_ref, v_ref, out_ref):
    cells = SBLK * SBLK
    for m in range(out_ref.shape[0]):
        u = u_ref[:, m * cells : (m + 1) * cells].astype(F32)
        v = v_ref[:, m * cells : (m + 1) * cells].astype(F32)
        cell_rows = jnp.concatenate([u[i : i + 1, :] * v for i in range(GRID)], axis=0)
        out_ref[m] = cell_rows.T.astype(BF)


def grid_weights(kern_u, kern_v):
    cells = SBLK * SBLK
    count = kern_u.shape[1] // cells
    step = math.gcd(count, 8)
    part = pl.BlockSpec((GRID, step * cells), lambda m: (0, m))
    return pl.pallas_call(
        weights_kernel,
        grid=(count // step,),
        out_shape=jax.ShapeDtypeStruct((count, cells, GRID * GRID), BF),
        in_specs=[part, part],
        out_specs=pl.BlockSpec((step, cells, GRID * GRID), lambda m: (m, 0, 0)),
        compiler_params=pltpu.CompilerParams(vmem_limit_bytes=16 << 20),
        cost_estimate=pl.CostEstimate(
            flops=count * GRID * GRID * cells, bytes_accessed=2 * count * GRID * GRID * cells, transcendentals=0
        ),
        name="grid_weights",
    )(kern_u, kern_v)


def correlate_kernel(sizes, slots_ref, r_ref, k_ref, out_ref, arr, vis, weights, acc, sem):
    owners, times, frames = sizes
    group2 = r_ref.shape[1]
    total = times * frames
    stations = owners * SBLK
    sides = stations // LANES
    arr_pitch = total + PAD
    vis_pitch = group2 + PAD
    fetch = pltpu.make_async_copy(k_ref, weights, sem)
    fetch.start()

    def turn(t, _):
        for tile in range(frames // 8):
            for side in range(sides):
                got = [
                    r_ref[(side * 8 + i) * times + t, :, tile * LANES : (tile + 1) * LANES]
                    for i in range(8)
                ]
                for i, w in enumerate(swap_groups(got)):
                    arr[side, pl.ds(t * frames + tile * 8 + i, group2, stride=arr_pitch), :] = w.astype(F32)
        return 0

    lax.fori_loop(0, times, turn, 0)

    def correlate(g, _):
        def part(side, c):
            at = pl.ds(pl.multiple_of((2 * g + c) * arr_pitch, 8), total)
            return arr[side, at, :].astype(BF)

        re = [part(side, 0) for side in range(sides)]
        im = [part(side, 1) for side in range(sides)]
        for side in range(sides):
            left = jnp.concatenate(
                [jnp.concatenate(re[: side + 1], axis=1), jnp.concatenate(im[: side + 1], axis=1)], axis=0
            )
            right = jnp.concatenate(
                [
                    jnp.concatenate([re[side], -im[side]], axis=1),
                    jnp.concatenate([im[side], re[side]], axis=1),
                ],
                axis=0,
            )
            z = lax.dot_general(left, right, TN, preferred_element_type=F32)
            for c in range(2):
                vis[side, pl.ds(2 * g + c, (side + 1) * LANES, stride=vis_pitch), :] = z[
                    :, c * LANES : (c + 1) * LANES
                ]
        return 0

    lax.fori_loop(0, group2 // 2, correlate, 0, unroll=8)

    acc[...] = jnp.zeros_like(acc)
    fetch.wait()

    m = 0
    for p in range(owners - 1):
        halves = {}
        for side in range(sides):
            if p >= side * 8 + 7:
                continue
            for half in range(2):
                got = [
                    vis[side, pl.ds((p * SBLK + half * 8 + i) * vis_pitch, group2), :].astype(BF)
                    for i in range(8)
                ]
                for i, w in enumerate(swap_groups(got)):
                    halves[side * 8 + i, half] = w
        for q in range(p + 1, owners):
            block = jnp.concatenate([halves[q, 0], halves[q, 1]], axis=1)
            z = jnp.dot(block, weights[m], preferred_element_type=F32)
            slot = slots_ref[m]
            acc[slot] = acc[slot] + z
            m += 1
    out_ref[...] = (acc[...] * (1.0 / math.sqrt(total))).astype(BF)


def correlate(turned, slots, weights, owners, times, frames, tiles):
    group2 = turned.shape[1]
    stations = owners * SBLK
    whole = pl.BlockSpec(memory_space=pltpu.VMEM)
    smem = pl.BlockSpec(memory_space=pltpu.SMEM)
    return pl.pallas_call(
        functools.partial(correlate_kernel, (owners, times, frames)),
        out_shape=jax.ShapeDtypeStruct((tiles, group2, GRID * GRID), BF),
        in_specs=[smem, whole, pl.BlockSpec(memory_space=pl.ANY)],
        out_specs=whole,
        scratch_shapes=[
            pltpu.VMEM((stations // LANES, group2 * (times * frames + PAD), LANES), F32),
            pltpu.VMEM((stations // LANES, stations * (group2 + PAD), LANES), F32),
            pltpu.VMEM(weights.shape, BF),
            pltpu.VMEM((tiles, group2, GRID * GRID), F32),
            pltpu.SemaphoreType.DMA,
        ],
        compiler_params=pltpu.CompilerParams(vmem_limit_bytes=42 << 20),
        name="correlate",
    )(slots, turned, weights)


def body(samples, taps, block_tile, tile_slots, kern_u, kern_v):
    frame_count = samples.shape[1]
    chan_size = lax.axis_size("chan")
    tm_size = lax.axis_size("tm")
    last, first = samples[:, frame_count - HALO :], samples[:, :HALO]
    before = lax.ppermute(last, "tm", [(i, i + 1) for i in range(tm_size - 1)])
    after = lax.ppermute(first, "tm", [((i + 1) % tm_size, i) for i in range(tm_size)])
    keep = (lax.axis_index("tm") < tm_size - 1).astype(F32).reshape(1)
    weights = grid_weights(kern_u, kern_v)
    pairs, ends = (jnp.asarray(table) for table in dft_tables(samples.shape[2]))
    done, part = channelize_own(keep, samples, taps, pairs, ends)
    spectra = channelize_rest(before, after, taps, pairs, ends, done, part)
    turned = lax.all_to_all(spectra, ("chan", "tm"), split_axis=0, concat_axis=0, tiled=True)
    tile_count = tile_slots.shape[0]
    slot_ids = jnp.arange(tile_count, dtype=jnp.int32)
    slots = jnp.sum(
        jnp.where(block_tile[:, None] == tile_slots[None, :], slot_ids[None, :], 0), axis=1
    )
    grids = correlate(turned, slots, weights, chan_size, tm_size, frame_count, tile_count)
    width = grids.shape[1] // 2
    partial_value = grids.reshape(tile_count, width, 2, GRID * GRID)
    return lax.all_to_all(partial_value, "tm", split_axis=0, concat_axis=1, tiled=True).astype(F32)


def solution(mesh):
    placed = (P("chan", "tm", None), P(), P(), P(), P(), P())
    return jax.shard_map(
        body, mesh=mesh, in_specs=placed, out_specs=P("tm", "chan", None, None), check_vma=False
    )
```

```python
import functools
import math

import jax
import jax.numpy as jnp
import ml_dtypes
import numpy as np
from jax import lax
from jax.experimental import pallas as pl
from jax.experimental.pallas import tpu as pltpu
from jax.sharding import PartitionSpec as P

SBLK = 16
GRID = 16
RADIX = 16
HALO = 8
PITCH = 24
PAD = 8
PIECES = 4
LANES = 128
BF = jnp.bfloat16
F32 = jnp.float32
NT = (((1,), (1,)), ((), ()))
TN = (((0,), (0,)), ((), ()))


def dft_tables(length):
    span = length // RADIX
    place = np.arange(span)[None, :]
    dest = np.arange(length // (2 * RADIX))[:, None]

    def table(low):
        angle = (place * (low + RADIX * dest) % length) * (2.0 * np.pi / length)
        c, s = np.cos(angle), np.sin(angle)
        sign = -1.0 if low > RADIX // 2 else 1.0
        return np.block([[c, sign * s], [-s, sign * c]]) / math.sqrt(length)

    pairs = np.stack(
        [np.concatenate([table(k), table(RADIX - k)], axis=0) for k in range(1, RADIX // 2)]
    )
    ends = np.stack([table(0)[:, :span], table(RADIX // 2)[:, :span]])
    return pairs.astype(ml_dtypes.bfloat16), ends.astype(ml_dtypes.bfloat16)


def real_dft(x):
    n = len(x)
    if n == 2:
        return [(x[0] + x[1], None), (x[0] - x[1], None)]
    even, odd = real_dft(x[0::2]), real_dft(x[1::2])
    out = [None] * (n // 2 + 1)
    for k in range(n // 4 + 1):
        er, ei = even[k]
        dr, di = odd[k]
        if k == 0:
            out[0], out[n // 2] = (er + dr, None), (er - dr, None)
        elif k == n // 4:
            out[k] = (er, -dr)
        else:
            c, s = math.cos(2 * math.pi * k / n), math.sin(2 * math.pi * k / n)
            if 8 * k == n:
                tr, ti = (dr + di) * c, (di - dr) * c
            else:
                tr, ti = dr * c + di * s, di * c - dr * s
            out[k] = (er + tr, ei + ti)
            out[n // 2 - k] = (er - tr, ti - ei)
    return out


def spread(source, target, first, at):
    for s in range(source.shape[0]):
        target[pl.ds(first * PITCH + s, source.shape[1], stride=PITCH), :] = source[s, :, at].astype(F32)


def butterflies(filt, low, half):
    to = slice(half * LANES, (half + 1) * LANES)

    def butterfly(b, _):
        at = pl.ds(pl.multiple_of(b * SBLK, SBLK), SBLK)
        parts = real_dft([filt[tile, at, :].astype(F32) for tile in range(RADIX)])
        for k, (re, im) in enumerate(parts):
            low[k, at, to] = re.astype(BF)
            if im is not None:
                low[RADIX // 2 + k, at, to] = im.astype(BF)
        return 0

    lax.fori_loop(0, filt.shape[1] // SBLK, butterfly, 0, unroll=2)


def products(low, turned, pairs_ref, ends_ref):
    dests = ends_ref.shape[1] // 2
    pitch = 2 * RADIX + PAD

    def keep(channel, part, value):
        for tile in range(low.shape[1] // LANES):
            turned[tile, pl.ds(channel * 2 + part, dests, stride=pitch), :] = value[
                :, tile * LANES : (tile + 1) * LANES
            ]

    for end in range(2):
        z = lax.dot_general(
            ends_ref[end], low[end * (RADIX // 2)], NT, preferred_element_type=F32
        )
        for part in range(2):
            keep(end * (RADIX // 2), part, z[part * dests : (part + 1) * dests])

    def pair(k, _):
        spectrum = jnp.concatenate([low[k], low[RADIX // 2 + k]], axis=1)
        for mirrored in range(2):
            z = lax.dot_general(
                pairs_ref[k - 1, mirrored * 2 * dests : (mirrored + 1) * 2 * dests, :],
                spectrum,
                NT,
                preferred_element_type=F32,
            )
            channel = RADIX - k if mirrored else k
            for part in range(2):
                keep(channel, part, z[part * dests : (part + 1) * dests])
        return 0

    lax.fori_loop(1, RADIX // 2, pair, 0, unroll=RADIX // 2 - 1)


def own_kernel(
    keep_ref,
    x_hbm,
    taps_ref,
    pairs_hbm,
    ends_hbm,
    out_ref,
    part_ref,
    xs,
    filt,
    low,
    turned,
    x_ref,
    pairs_ref,
    ends_ref,
    sems,
):
    samples = pltpu.make_async_copy(x_hbm, x_ref, sems.at[2])
    samples.start()
    fetches = [
        pltpu.make_async_copy(pairs_hbm, pairs_ref, sems.at[0]),
        pltpu.make_async_copy(ends_hbm, ends_ref, sems.at[1]),
    ]
    for fetch in fetches:
        fetch.start()
    stations, frames, length = x_ref.shape
    taps = taps_ref.shape[0]
    span = length // RADIX
    own = keep_ref[0]
    done = range(HALO, 2 * HALO)
    samples.wait()

    for half in range(span // LANES):

        def fir(tile, _):
            at = pl.ds(pl.multiple_of(tile * span + half * LANES, LANES), LANES)
            spread(x_ref, xs, 0, at)
            weights = [taps_ref[pl.ds(k, 1), at] for k in range(taps)]
            sums = {}
            for step in range(frames):
                x = xs[step * PITCH : step * PITCH + stations, :]
                for k in range(taps - 1, -1, -1):
                    b = step + HALO - (taps - 1) + k
                    if 0 <= b < frames:
                        term = weights[k] * x
                        sums[b] = sums[b] + term if b in sums else term
                ready = [b for b in sums if b == step + HALO - (taps - 1) or step == frames - 1]
                for b in ready:
                    value = sums.pop(b)
                    if b in done:
                        place = b - done.start
                        filt[tile, place * stations : (place + 1) * stations, :] = value.astype(BF)
                    else:
                        place = b if b < done.start else b - len(done)
                        if b + taps - 1 >= HALO + frames:
                            value = own * value
                        part_ref[2 * tile + half, place * stations : (place + 1) * stations, :] = value
            return 0

        lax.fori_loop(0, RADIX, fir, 0)
        butterflies(filt, low, half)

    for fetch in fetches:
        fetch.wait()
    products(low, turned, pairs_ref, ends_ref)

    def give(d, _):
        at = pl.ds(pl.multiple_of(d * (2 * RADIX + PAD), 8), 2 * RADIX)
        out_ref[d] = turned[0, at, :].astype(BF)
        return 0

    lax.fori_loop(0, out_ref.shape[0], give, 0, unroll=8)


def rest_kernel(
    left_ref, right_ref, taps_ref, pairs_ref, ends_ref, done_ref, part_ref, out_hbm, xs, filt, low, turned, stage, sems
):
    width = stage.shape[2]
    finished = pltpu.make_async_copy(done_ref, out_hbm.at[:, :, width:], sems.at[PIECES])
    finished.start()
    stations, _, length = left_ref.shape
    taps = taps_ref.shape[0]
    span = length // RADIX
    count = part_ref.shape[1] // stations

    for half in range(span // LANES):

        def fir(tile, _):
            at = pl.ds(pl.multiple_of(tile * span + half * LANES, LANES), LANES)
            spread(left_ref, xs, 0, at)
            spread(right_ref, xs, HALO, at)
            weights = [taps_ref[pl.ds(k, 1), at] for k in range(taps)]
            x = [xs[step * PITCH : step * PITCH + stations, :] for step in range(2 * HALO)]
            for place in range(count):
                to = slice(place * stations, (place + 1) * stations)
                value = part_ref[2 * tile + half, to, :]
                if place < HALO:
                    terms = [(j, taps - 1 - (j - place)) for j in range(place, HALO)]
                else:
                    first = place - (count - (HALO - 1))
                    terms = [(HALO + j, first - j) for j in range(first + 1)]
                for j, k in terms:
                    value = value + weights[k] * x[j]
                filt[tile, to, :] = value.astype(BF)
            return 0

        lax.fori_loop(0, RADIX, fir, 0)
        butterflies(filt, low, half)

    products(low, turned, pairs_ref, ends_ref)
    count = stage.shape[0] // PIECES
    copies = []
    for piece in range(PIECES):

        def give(d, _):
            at = pl.ds(pl.multiple_of(d * (2 * RADIX + PAD), 8), 2 * RADIX)
            for tile in range(width // LANES):
                stage[d, :, tile * LANES : (tile + 1) * LANES] = turned[tile, at, :].astype(BF)
            return 0

        lax.fori_loop(piece * count, (piece + 1) * count, give, 0, unroll=8)
        to = pl.ds(piece * count, count)
        copy = pltpu.make_async_copy(stage.at[to], out_hbm.at[to, :, :width], sems.at[piece])
        copy.start()
        copies.append(copy)
    for copy in copies + [finished]:
        copy.wait()


def channel_scratch(frames, steps, length):
    rows = frames * SBLK
    return [
        pltpu.VMEM((steps * PITCH, LANES), F32),
        pltpu.VMEM((RADIX, rows, LANES), BF),
        pltpu.VMEM((RADIX, rows, length // RADIX), BF),
        pltpu.VMEM((rows // LANES, length // (2 * RADIX) * (2 * RADIX + PAD), LANES), F32),
    ]


def channelize_own(keep, samples, taps, pairs, ends):
    stations, frames, length = samples.shape
    dests = length // (2 * RADIX)
    whole = pl.BlockSpec(memory_space=pltpu.VMEM)
    return pl.pallas_call(
        own_kernel,
        out_shape=[
            jax.ShapeDtypeStruct((dests, 2 * RADIX, HALO * stations), BF),
            jax.ShapeDtypeStruct((length // LANES, (frames - HALO) * stations, LANES), F32),
        ],
        in_specs=[pl.BlockSpec(memory_space=pltpu.SMEM)]
        + [pl.BlockSpec(memory_space=pltpu.HBM), whole]
        + [pl.BlockSpec(memory_space=pltpu.HBM)] * 2,
        out_specs=[whole] * 2,
        scratch_shapes=channel_scratch(HALO, frames, length)
        + [
            pltpu.VMEM(samples.shape, BF),
            pltpu.VMEM(pairs.shape, BF),
            pltpu.VMEM(ends.shape, BF),
            pltpu.SemaphoreType.DMA((3,)),
        ],
        compiler_params=pltpu.CompilerParams(vmem_limit_bytes=22 << 20),
        cost_estimate=pl.CostEstimate(
            flops=10 * samples.size * 1000, bytes_accessed=20 << 20, transcendentals=0
        ),
        name="own",
    )(
        keep,
        pltpu.with_memory_space_constraint(samples, pltpu.HBM),
        taps,
        pltpu.with_memory_space_constraint(pairs, pltpu.HBM),
        pltpu.with_memory_space_constraint(ends, pltpu.HBM),
    )


def channelize_rest(before, after, taps, pairs, ends, done, part):
    stations, _, length = before.shape
    dests = length // (2 * RADIX)
    frames = part.shape[1] // stations
    whole = pl.BlockSpec(memory_space=pltpu.VMEM)
    return pl.pallas_call(
        rest_kernel,
        out_shape=jax.ShapeDtypeStruct((dests, 2 * RADIX, part.shape[1] + done.shape[2]), BF),
        in_specs=[whole] * 7,
        out_specs=pl.BlockSpec(memory_space=pltpu.HBM),
        scratch_shapes=channel_scratch(frames, 2 * HALO, length)
        + [
            pltpu.VMEM((dests, 2 * RADIX, part.shape[1]), BF),
            pltpu.SemaphoreType.DMA((PIECES + 1,)),
        ],
        compiler_params=pltpu.CompilerParams(vmem_limit_bytes=28 << 20),
        name="rest",
    )(before, after, taps, pairs, ends, done, part)


def swap_groups(v):
    group = lax.broadcasted_iota(jnp.int32, v[0].shape, 1) // SBLK
    v = [pltpu.roll(a, i * SBLK, 1) if i else a for i, a in enumerate(v)]
    v = [v[-i % 8] for i in range(8)]
    for bit in (1, 2, 4):
        odd = (group & bit) != 0
        v = [jnp.where(odd, v[(i - bit) % 8], v[i]) for i in range(8)]
    return [pltpu.roll(a, LANES - j * SBLK, 1) if j else a for j, a in enumerate(v)]


def weights_kernel(u_ref, v_ref, out_ref):
    cells = SBLK * SBLK
    for m in range(out_ref.shape[0]):
        u = u_ref[:, m * cells : (m + 1) * cells].astype(F32)
        v = v_ref[:, m * cells : (m + 1) * cells].astype(F32)
        cell_rows = jnp.concatenate([u[i : i + 1, :] * v for i in range(GRID)], axis=0)
        out_ref[m] = cell_rows.T.astype(BF)


def grid_weights(kern_u, kern_v):
    cells = SBLK * SBLK
    count = kern_u.shape[1] // cells
    step = math.gcd(count, 8)
    part = pl.BlockSpec((GRID, step * cells), lambda m: (0, m))
    return pl.pallas_call(
        weights_kernel,
        grid=(count // step,),
        out_shape=jax.ShapeDtypeStruct((count, cells, GRID * GRID), BF),
        in_specs=[part, part],
        out_specs=pl.BlockSpec((step, cells, GRID * GRID), lambda m: (m, 0, 0)),
        compiler_params=pltpu.CompilerParams(vmem_limit_bytes=16 << 20),
        cost_estimate=pl.CostEstimate(
            flops=count * GRID * GRID * cells, bytes_accessed=2 * count * GRID * GRID * cells, transcendentals=0
        ),
        name="grid_weights",
    )(kern_u, kern_v)


def correlate_kernel(sizes, slots_ref, r_ref, k_ref, out_ref, arr, vis, weights, acc, sem):
    owners, times, frames = sizes
    group2 = r_ref.shape[1]
    total = times * frames
    stations = owners * SBLK
    sides = stations // LANES
    arr_pitch = total + PAD
    vis_pitch = group2 + PAD
    fetch = pltpu.make_async_copy(k_ref, weights, sem)
    fetch.start()

    def turn(t, _):
        for tile in range(frames // 8):
            for side in range(sides):
                got = [
                    r_ref[(side * 8 + i) * times + t, :, tile * LANES : (tile + 1) * LANES]
                    for i in range(8)
                ]
                for i, w in enumerate(swap_groups(got)):
                    arr[side, pl.ds(t * frames + tile * 8 + i, group2, stride=arr_pitch), :] = w.astype(F32)
        return 0

    lax.fori_loop(0, times, turn, 0)

    def correlate(g, _):
        def part(side, c):
            at = pl.ds(pl.multiple_of((2 * g + c) * arr_pitch, 8), total)
            return arr[side, at, :].astype(BF)

        re = [part(side, 0) for side in range(sides)]
        im = [part(side, 1) for side in range(sides)]
        for side in range(sides):
            left = jnp.concatenate(
                [jnp.concatenate(re[: side + 1], axis=1), jnp.concatenate(im[: side + 1], axis=1)], axis=0
            )
            right = jnp.concatenate(
                [
                    jnp.concatenate([re[side], -im[side]], axis=1),
                    jnp.concatenate([im[side], re[side]], axis=1),
                ],
                axis=0,
            )
            z = lax.dot_general(left, right, TN, preferred_element_type=F32)
            for c in range(2):
                vis[side, pl.ds(2 * g + c, (side + 1) * LANES, stride=vis_pitch), :] = z[
                    :, c * LANES : (c + 1) * LANES
                ]
        return 0

    lax.fori_loop(0, group2 // 2, correlate, 0, unroll=8)

    acc[...] = jnp.zeros_like(acc)
    fetch.wait()

    m = 0
    for p in range(owners - 1):
        halves = {}
        for side in range(sides):
            if p >= side * 8 + 7:
                continue
            for half in range(2):
                got = [
                    vis[side, pl.ds((p * SBLK + half * 8 + i) * vis_pitch, group2), :].astype(BF)
                    for i in range(8)
                ]
                for i, w in enumerate(swap_groups(got)):
                    halves[side * 8 + i, half] = w
        for q in range(p + 1, owners):
            block = jnp.concatenate([halves[q, 0], halves[q, 1]], axis=1)
            z = jnp.dot(block, weights[m], preferred_element_type=F32)
            slot = slots_ref[m]
            acc[slot] = acc[slot] + z
            m += 1
    out_ref[...] = (acc[...] * (1.0 / math.sqrt(total))).astype(BF)


def correlate(turned, slots, weights, owners, times, frames, tiles):
    group2 = turned.shape[1]
    stations = owners * SBLK
    whole = pl.BlockSpec(memory_space=pltpu.VMEM)
    smem = pl.BlockSpec(memory_space=pltpu.SMEM)
    return pl.pallas_call(
        functools.partial(correlate_kernel, (owners, times, frames)),
        out_shape=jax.ShapeDtypeStruct((tiles, group2, GRID * GRID), BF),
        in_specs=[smem, whole, pl.BlockSpec(memory_space=pl.ANY)],
        out_specs=whole,
        scratch_shapes=[
            pltpu.VMEM((stations // LANES, group2 * (times * frames + PAD), LANES), F32),
            pltpu.VMEM((stations // LANES, stations * (group2 + PAD), LANES), F32),
            pltpu.VMEM(weights.shape, BF),
            pltpu.VMEM((tiles, group2, GRID * GRID), F32),
            pltpu.SemaphoreType.DMA,
        ],
        compiler_params=pltpu.CompilerParams(vmem_limit_bytes=42 << 20),
        name="correlate",
    )(slots, turned, weights)


def body(samples, taps, block_tile, tile_slots, kern_u, kern_v):
    frame_count = samples.shape[1]
    chan_size = lax.axis_size("chan")
    tm_size = lax.axis_size("tm")
    last, first = samples[:, frame_count - HALO :], samples[:, :HALO]
    before = lax.ppermute(last, "tm", [(i, i + 1) for i in range(tm_size - 1)])
    after = lax.ppermute(first, "tm", [((i + 1) % tm_size, i) for i in range(tm_size)])
    keep = (lax.axis_index("tm") < tm_size - 1).astype(F32).reshape(1)
    weights = grid_weights(kern_u, kern_v)
    pairs, ends = (jnp.asarray(table) for table in dft_tables(samples.shape[2]))
    done, part = channelize_own(keep, samples, taps, pairs, ends)
    spectra = channelize_rest(before, after, taps, pairs, ends, done, part)
    turned = lax.all_to_all(spectra, ("chan", "tm"), split_axis=0, concat_axis=0, tiled=True)
    tile_count = tile_slots.shape[0]
    slot_ids = jnp.arange(tile_count, dtype=jnp.int32)
    slots = jnp.sum(
        jnp.where(block_tile[:, None] == tile_slots[None, :], slot_ids[None, :], 0), axis=1
    )
    grids = correlate(turned, slots, weights, chan_size, tm_size, frame_count, tile_count)
    width = grids.shape[1] // 2
    partial_value = grids.reshape(tile_count, width, 2, GRID * GRID)
    return lax.all_to_all(partial_value, "tm", split_axis=0, concat_axis=1, tiled=True).astype(F32)


def solution(mesh):
    placed = (P("chan", "tm", None), P(), P(), P(), P(), P())
    return jax.shard_map(
        body, mesh=mesh, in_specs=placed, out_specs=P("tm", "chan", None, None), check_vma=False
    )
```

```python
import functools
import math

import jax
import jax.numpy as jnp
import ml_dtypes
import numpy as np
from jax import lax
from jax.experimental import pallas as pl
from jax.experimental.pallas import tpu as pltpu
from jax.sharding import PartitionSpec as P

SBLK = 16
GRID = 16
RADIX = 16
HALO = 8
PITCH = 24
PAD = 8
PIECES = 4
LANES = 128
BF = jnp.bfloat16
F32 = jnp.float32
NT = (((1,), (1,)), ((), ()))
TN = (((0,), (0,)), ((), ()))


def dft_tables(length):
    span = length // RADIX
    place = np.arange(span)[None, :]
    dest = np.arange(length // (2 * RADIX))[:, None]

    def table(low):
        angle = (place * (low + RADIX * dest) % length) * (2.0 * np.pi / length)
        c, s = np.cos(angle), np.sin(angle)
        sign = -1.0 if low > RADIX // 2 else 1.0
        return np.block([[c, sign * s], [-s, sign * c]]) / math.sqrt(length)

    pairs = np.stack(
        [np.concatenate([table(k), table(RADIX - k)], axis=0) for k in range(1, RADIX // 2)]
    )
    ends = np.stack([table(0)[:, :span], table(RADIX // 2)[:, :span]])
    return pairs.astype(ml_dtypes.bfloat16), ends.astype(ml_dtypes.bfloat16)


def real_dft(x):
    n = len(x)
    if n == 2:
        return [(x[0] + x[1], None), (x[0] - x[1], None)]
    even, odd = real_dft(x[0::2]), real_dft(x[1::2])
    out = [None] * (n // 2 + 1)
    for k in range(n // 4 + 1):
        er, ei = even[k]
        dr, di = odd[k]
        if k == 0:
            out[0], out[n // 2] = (er + dr, None), (er - dr, None)
        elif k == n // 4:
            out[k] = (er, -dr)
        else:
            c, s = math.cos(2 * math.pi * k / n), math.sin(2 * math.pi * k / n)
            if 8 * k == n:
                tr, ti = (dr + di) * c, (di - dr) * c
            else:
                tr, ti = dr * c + di * s, di * c - dr * s
            out[k] = (er + tr, ei + ti)
            out[n // 2 - k] = (er - tr, ti - ei)
    return out


def spread(source, target, first, at):
    for s in range(source.shape[0]):
        target[pl.ds(first * PITCH + s, source.shape[1], stride=PITCH), :] = source[s, :, at].astype(F32)


def butterflies(filt, low):
    def butterfly(b, _):
        at = pl.ds(pl.multiple_of(b * SBLK, SBLK), SBLK)
        for half in range(filt.shape[2] // LANES):
            to = slice(half * LANES, (half + 1) * LANES)
            parts = real_dft([filt[tile, at, to].astype(F32) for tile in range(RADIX)])
            for k, (re, im) in enumerate(parts):
                low[k, at, to] = re.astype(BF)
                if im is not None:
                    low[RADIX // 2 + k, at, to] = im.astype(BF)
        return 0

    lax.fori_loop(0, filt.shape[1] // SBLK, butterfly, 0)


def products(low, turned, pairs_ref, ends_ref):
    dests = ends_ref.shape[1] // 2
    pitch = 2 * RADIX + PAD

    def keep(channel, part, value):
        for tile in range(low.shape[1] // LANES):
            turned[tile, pl.ds(channel * 2 + part, dests, stride=pitch), :] = value[
                :, tile * LANES : (tile + 1) * LANES
            ]

    for end in range(2):
        z = lax.dot_general(
            ends_ref[end], low[end * (RADIX // 2)], NT, preferred_element_type=F32
        )
        for part in range(2):
            keep(end * (RADIX // 2), part, z[part * dests : (part + 1) * dests])

    def pair(k, _):
        spectrum = jnp.concatenate([low[k], low[RADIX // 2 + k]], axis=1)
        for mirrored in range(2):
            z = lax.dot_general(
                pairs_ref[k - 1, mirrored * 2 * dests : (mirrored + 1) * 2 * dests, :],
                spectrum,
                NT,
                preferred_element_type=F32,
            )
            channel = RADIX - k if mirrored else k
            for part in range(2):
                keep(channel, part, z[part * dests : (part + 1) * dests])
        return 0

    lax.fori_loop(1, RADIX // 2, pair, 0, unroll=RADIX // 2 - 1)


def own_kernel(
    keep_ref,
    x_hbm,
    taps_ref,
    pairs_hbm,
    ends_hbm,
    out_ref,
    part_ref,
    xs,
    filt,
    low,
    turned,
    x_ref,
    pairs_ref,
    ends_ref,
    sems,
):
    piece = x_hbm.shape[2] // PIECES
    samples = []
    for i in range(PIECES):
        part = (slice(None), slice(None), pl.ds(i * piece, piece))
        samples.append(pltpu.make_async_copy(x_hbm.at[part], x_ref.at[part], sems.at[2 + i]))
        samples[i].start()
    fetches = [
        pltpu.make_async_copy(pairs_hbm, pairs_ref, sems.at[0]),
        pltpu.make_async_copy(ends_hbm, ends_ref, sems.at[1]),
    ]
    for fetch in fetches:
        fetch.start()
    stations, frames, length = x_ref.shape
    taps = taps_ref.shape[0]
    span = length // RADIX
    own = keep_ref[0]
    done = range(HALO, 2 * HALO)

    def fir(tile, _):
        for half in range(span // LANES):
            at = pl.ds(pl.multiple_of(tile * span + half * LANES, LANES), LANES)
            spread(x_ref, xs, 0, at)
            weights = [taps_ref[pl.ds(k, 1), at] for k in range(taps)]
            sums = {}
            for step in range(frames):
                x = xs[step * PITCH : step * PITCH + stations, :]
                for k in range(taps - 1, -1, -1):
                    b = step + HALO - (taps - 1) + k
                    if 0 <= b < frames:
                        term = weights[k] * x
                        sums[b] = sums[b] + term if b in sums else term
                ready = [b for b in sums if b == step + HALO - (taps - 1) or step == frames - 1]
                for b in ready:
                    value = sums.pop(b)
                    if b in done:
                        place = b - done.start
                        to = slice(half * LANES, (half + 1) * LANES)
                        filt[tile, place * stations : (place + 1) * stations, to] = value.astype(BF)
                    else:
                        place = b if b < done.start else b - len(done)
                        if b + taps - 1 >= HALO + frames:
                            value = own * value
                        part_ref[2 * tile + half, place * stations : (place + 1) * stations, :] = value
        return 0

    for i in range(PIECES):
        samples[i].wait()
        lax.fori_loop(i * RADIX // PIECES, (i + 1) * RADIX // PIECES, fir, 0)
    butterflies(filt, low)
    for fetch in fetches:
        fetch.wait()
    products(low, turned, pairs_ref, ends_ref)

    def give(d, _):
        at = pl.ds(pl.multiple_of(d * (2 * RADIX + PAD), 8), 2 * RADIX)
        out_ref[d] = turned[0, at, :].astype(BF)
        return 0

    lax.fori_loop(0, out_ref.shape[0], give, 0, unroll=8)


def rest_kernel(
    left_ref, right_ref, taps_ref, pairs_ref, ends_ref, done_ref, part_ref, out_hbm, xs, filt, low, turned, stage, sems
):
    width = stage.shape[2]
    finished = pltpu.make_async_copy(done_ref, out_hbm.at[:, :, width:], sems.at[PIECES])
    finished.start()
    stations, _, length = left_ref.shape
    taps = taps_ref.shape[0]
    span = length // RADIX
    count = part_ref.shape[1] // stations

    def fir(tile, _):
        for half in range(span // LANES):
            at = pl.ds(pl.multiple_of(tile * span + half * LANES, LANES), LANES)
            lanes = slice(half * LANES, (half + 1) * LANES)
            spread(left_ref, xs, 0, at)
            spread(right_ref, xs, HALO, at)
            weights = [taps_ref[pl.ds(k, 1), at] for k in range(taps)]
            x = [xs[step * PITCH : step * PITCH + stations, :] for step in range(2 * HALO)]
            for place in range(count):
                to = slice(place * stations, (place + 1) * stations)
                value = part_ref[2 * tile + half, to, :]
                if place < HALO:
                    terms = [(j, taps - 1 - (j - place)) for j in range(place, HALO)]
                else:
                    first = place - (count - (HALO - 1))
                    terms = [(HALO + j, first - j) for j in range(first + 1)]
                for j, k in terms:
                    value = value + weights[k] * x[j]
                filt[tile, to, lanes] = value.astype(BF)
        return 0

    lax.fori_loop(0, RADIX, fir, 0)
    butterflies(filt, low)
    products(low, turned, pairs_ref, ends_ref)
    count = stage.shape[0] // PIECES
    copies = []
    for piece in range(PIECES):

        def give(d, _):
            at = pl.ds(pl.multiple_of(d * (2 * RADIX + PAD), 8), 2 * RADIX)
            for tile in range(width // LANES):
                stage[d, :, tile * LANES : (tile + 1) * LANES] = turned[tile, at, :].astype(BF)
            return 0

        lax.fori_loop(piece * count, (piece + 1) * count, give, 0, unroll=8)
        to = pl.ds(piece * count, count)
        copy = pltpu.make_async_copy(stage.at[to], out_hbm.at[to, :, :width], sems.at[piece])
        copy.start()
        copies.append(copy)
    for copy in copies + [finished]:
        copy.wait()


def channel_scratch(frames, steps, length):
    rows = frames * SBLK
    return [
        pltpu.VMEM((steps * PITCH, LANES), F32),
        pltpu.VMEM((RADIX, rows, length // RADIX), BF),
        pltpu.VMEM((RADIX, rows, length // RADIX), BF),
        pltpu.VMEM((rows // LANES, length // (2 * RADIX) * (2 * RADIX + PAD), LANES), F32),
    ]


def channelize_own(keep, samples, taps, pairs, ends):
    stations, frames, length = samples.shape
    dests = length // (2 * RADIX)
    whole = pl.BlockSpec(memory_space=pltpu.VMEM)
    return pl.pallas_call(
        own_kernel,
        out_shape=[
            jax.ShapeDtypeStruct((dests, 2 * RADIX, HALO * stations), BF),
            jax.ShapeDtypeStruct((length // LANES, (frames - HALO) * stations, LANES), F32),
        ],
        in_specs=[pl.BlockSpec(memory_space=pltpu.SMEM)]
        + [pl.BlockSpec(memory_space=pltpu.HBM), whole]
        + [pl.BlockSpec(memory_space=pltpu.HBM)] * 2,
        out_specs=[whole] * 2,
        scratch_shapes=channel_scratch(HALO, frames, length)
        + [
            pltpu.VMEM(samples.shape, BF),
            pltpu.VMEM(pairs.shape, BF),
            pltpu.VMEM(ends.shape, BF),
            pltpu.SemaphoreType.DMA((2 + PIECES,)),
        ],
        compiler_params=pltpu.CompilerParams(vmem_limit_bytes=22 << 20),
        cost_estimate=pl.CostEstimate(
            flops=10 * samples.size * 1000, bytes_accessed=20 << 20, transcendentals=0
        ),
        name="own",
    )(
        keep,
        pltpu.with_memory_space_constraint(samples, pltpu.HBM),
        taps,
        pltpu.with_memory_space_constraint(pairs, pltpu.HBM),
        pltpu.with_memory_space_constraint(ends, pltpu.HBM),
    )


def channelize_rest(before, after, taps, pairs, ends, done, part):
    stations, _, length = before.shape
    dests = length // (2 * RADIX)
    frames = part.shape[1] // stations
    whole = pl.BlockSpec(memory_space=pltpu.VMEM)
    return pl.pallas_call(
        rest_kernel,
        out_shape=jax.ShapeDtypeStruct((dests, 2 * RADIX, part.shape[1] + done.shape[2]), BF),
        in_specs=[whole] * 7,
        out_specs=pl.BlockSpec(memory_space=pltpu.HBM),
        scratch_shapes=channel_scratch(frames, 2 * HALO, length)
        + [
            pltpu.VMEM((dests, 2 * RADIX, part.shape[1]), BF),
            pltpu.SemaphoreType.DMA((PIECES + 1,)),
        ],
        compiler_params=pltpu.CompilerParams(vmem_limit_bytes=28 << 20),
        name="rest",
    )(before, after, taps, pairs, ends, done, part)


def swap_groups(v):
    group = lax.broadcasted_iota(jnp.int32, v[0].shape, 1) // SBLK
    v = [pltpu.roll(a, i * SBLK, 1) if i else a for i, a in enumerate(v)]
    v = [v[-i % 8] for i in range(8)]
    for bit in (1, 2, 4):
        odd = (group & bit) != 0
        v = [jnp.where(odd, v[(i - bit) % 8], v[i]) for i in range(8)]
    return [pltpu.roll(a, LANES - j * SBLK, 1) if j else a for j, a in enumerate(v)]


def weights_kernel(u_ref, v_ref, out_ref):
    cells = SBLK * SBLK
    for m in range(out_ref.shape[0]):
        u = u_ref[:, m * cells : (m + 1) * cells].astype(F32)
        v = v_ref[:, m * cells : (m + 1) * cells].astype(F32)
        cell_rows = jnp.concatenate([u[i : i + 1, :] * v for i in range(GRID)], axis=0)
        out_ref[m] = cell_rows.T.astype(BF)


def grid_weights(kern_u, kern_v):
    cells = SBLK * SBLK
    count = kern_u.shape[1] // cells
    step = math.gcd(count, 8)
    part = pl.BlockSpec((GRID, step * cells), lambda m: (0, m))
    return pl.pallas_call(
        weights_kernel,
        grid=(count // step,),
        out_shape=jax.ShapeDtypeStruct((count, cells, GRID * GRID), BF),
        in_specs=[part, part],
        out_specs=pl.BlockSpec((step, cells, GRID * GRID), lambda m: (m, 0, 0)),
        compiler_params=pltpu.CompilerParams(vmem_limit_bytes=16 << 20),
        cost_estimate=pl.CostEstimate(
            flops=count * GRID * GRID * cells, bytes_accessed=2 * count * GRID * GRID * cells, transcendentals=0
        ),
        name="grid_weights",
    )(kern_u, kern_v)


def correlate_kernel(sizes, slots_ref, r_ref, k_ref, out_ref, arr, vis, weights, acc, sem):
    owners, times, frames = sizes
    group2 = r_ref.shape[1]
    total = times * frames
    stations = owners * SBLK
    sides = stations // LANES
    arr_pitch = total + PAD
    vis_pitch = group2 + PAD
    fetch = pltpu.make_async_copy(k_ref, weights, sem)
    fetch.start()

    def turn(t, _):
        for tile in range(frames // 8):
            for side in range(sides):
                got = [
                    r_ref[(side * 8 + i) * times + t, :, tile * LANES : (tile + 1) * LANES]
                    for i in range(8)
                ]
                for i, w in enumerate(swap_groups(got)):
                    arr[side, pl.ds(t * frames + tile * 8 + i, group2, stride=arr_pitch), :] = w.astype(F32)
        return 0

    lax.fori_loop(0, times, turn, 0)

    def correlate(g, _):
        def part(side, c):
            at = pl.ds(pl.multiple_of((2 * g + c) * arr_pitch, 8), total)
            return arr[side, at, :].astype(BF)

        re = [part(side, 0) for side in range(sides)]
        im = [part(side, 1) for side in range(sides)]
        for side in range(sides):
            left = jnp.concatenate(
                [jnp.concatenate(re[: side + 1], axis=1), jnp.concatenate(im[: side + 1], axis=1)], axis=0
            )
            right = jnp.concatenate(
                [
                    jnp.concatenate([re[side], -im[side]], axis=1),
                    jnp.concatenate([im[side], re[side]], axis=1),
                ],
                axis=0,
            )
            z = lax.dot_general(left, right, TN, preferred_element_type=F32)
            for c in range(2):
                vis[side, pl.ds(2 * g + c, (side + 1) * LANES, stride=vis_pitch), :] = z[
                    :, c * LANES : (c + 1) * LANES
                ]
        return 0

    lax.fori_loop(0, group2 // 2, correlate, 0, unroll=8)

    acc[...] = jnp.zeros_like(acc)
    fetch.wait()

    m = 0
    for p in range(owners - 1):
        halves = {}
        for side in range(sides):
            if p >= side * 8 + 7:
                continue
            for half in range(2):
                got = [
                    vis[side, pl.ds((p * SBLK + half * 8 + i) * vis_pitch, group2), :].astype(BF)
                    for i in range(8)
                ]
                for i, w in enumerate(swap_groups(got)):
                    halves[side * 8 + i, half] = w
        for q in range(p + 1, owners):
            block = jnp.concatenate([halves[q, 0], halves[q, 1]], axis=1)
            z = jnp.dot(block, weights[m], preferred_element_type=F32)
            slot = slots_ref[m]
            acc[slot] = acc[slot] + z
            m += 1
    out_ref[...] = (acc[...] * (1.0 / math.sqrt(total))).astype(BF)


def correlate(turned, slots, weights, owners, times, frames, tiles):
    group2 = turned.shape[1]
    stations = owners * SBLK
    whole = pl.BlockSpec(memory_space=pltpu.VMEM)
    smem = pl.BlockSpec(memory_space=pltpu.SMEM)
    return pl.pallas_call(
        functools.partial(correlate_kernel, (owners, times, frames)),
        out_shape=jax.ShapeDtypeStruct((tiles, group2, GRID * GRID), BF),
        in_specs=[smem, whole, pl.BlockSpec(memory_space=pl.ANY)],
        out_specs=whole,
        scratch_shapes=[
            pltpu.VMEM((stations // LANES, group2 * (times * frames + PAD), LANES), F32),
            pltpu.VMEM((stations // LANES, stations * (group2 + PAD), LANES), F32),
            pltpu.VMEM(weights.shape, BF),
            pltpu.VMEM((tiles, group2, GRID * GRID), F32),
            pltpu.SemaphoreType.DMA,
        ],
        compiler_params=pltpu.CompilerParams(vmem_limit_bytes=42 << 20),
        name="correlate",
    )(slots, turned, weights)


def body(samples, taps, block_tile, tile_slots, kern_u, kern_v):
    frame_count = samples.shape[1]
    chan_size = lax.axis_size("chan")
    tm_size = lax.axis_size("tm")
    last, first = samples[:, frame_count - HALO :], samples[:, :HALO]
    before = lax.ppermute(last, "tm", [(i, i + 1) for i in range(tm_size - 1)])
    after = lax.ppermute(first, "tm", [((i + 1) % tm_size, i) for i in range(tm_size)])
    keep = (lax.axis_index("tm") < tm_size - 1).astype(F32).reshape(1)
    weights = grid_weights(kern_u, kern_v)
    pairs, ends = (jnp.asarray(table) for table in dft_tables(samples.shape[2]))
    done, part = channelize_own(keep, samples, taps, pairs, ends)
    spectra = channelize_rest(before, after, taps, pairs, ends, done, part)
    turned = lax.all_to_all(spectra, ("chan", "tm"), split_axis=0, concat_axis=0, tiled=True)
    tile_count = tile_slots.shape[0]
    slot_ids = jnp.arange(tile_count, dtype=jnp.int32)
    slots = jnp.sum(
        jnp.where(block_tile[:, None] == tile_slots[None, :], slot_ids[None, :], 0), axis=1
    )
    grids = correlate(turned, slots, weights, chan_size, tm_size, frame_count, tile_count)
    width = grids.shape[1] // 2
    partial_value = grids.reshape(tile_count, width, 2, GRID * GRID)
    return lax.all_to_all(partial_value, "tm", split_axis=0, concat_axis=1, tiled=True).astype(F32)


def solution(mesh):
    placed = (P("chan", "tm", None), P(), P(), P(), P(), P())
    return jax.shard_map(
        body, mesh=mesh, in_specs=placed, out_specs=P("tm", "chan", None, None), check_vma=False
    )
```

```python
import functools
import math

import jax
import jax.numpy as jnp
import ml_dtypes
import numpy as np
from jax import lax
from jax.experimental import pallas as pl
from jax.experimental.pallas import tpu as pltpu
from jax.sharding import PartitionSpec as P

SBLK = 16
GRID = 16
RADIX = 16
HALO = 8
PITCH = 24
PAD = 8
PIECES = 4
LANES = 128
BF = jnp.bfloat16
F32 = jnp.float32
NT = (((1,), (1,)), ((), ()))
TN = (((0,), (0,)), ((), ()))


def dft_tables(length):
    span = length // RADIX
    place = np.arange(span)[None, :]
    dest = np.arange(length // (2 * RADIX))[:, None]

    def table(low):
        angle = (place * (low + RADIX * dest) % length) * (2.0 * np.pi / length)
        c, s = np.cos(angle), np.sin(angle)
        sign = -1.0 if low > RADIX // 2 else 1.0
        return np.block([[c, sign * s], [-s, sign * c]]) / math.sqrt(length)

    pairs = np.stack(
        [np.concatenate([table(k), table(RADIX - k)], axis=0) for k in range(1, RADIX // 2)]
    )
    ends = np.stack([table(0)[:, :span], table(RADIX // 2)[:, :span]])
    return pairs.astype(ml_dtypes.bfloat16), ends.astype(ml_dtypes.bfloat16)


def real_dft(x):
    n = len(x)
    if n == 2:
        return [(x[0] + x[1], None), (x[0] - x[1], None)]
    even, odd = real_dft(x[0::2]), real_dft(x[1::2])
    out = [None] * (n // 2 + 1)
    for k in range(n // 4 + 1):
        er, ei = even[k]
        dr, di = odd[k]
        if k == 0:
            out[0], out[n // 2] = (er + dr, None), (er - dr, None)
        elif k == n // 4:
            out[k] = (er, -dr)
        else:
            c, s = math.cos(2 * math.pi * k / n), math.sin(2 * math.pi * k / n)
            if 8 * k == n:
                tr, ti = (dr + di) * c, (di - dr) * c
            else:
                tr, ti = dr * c + di * s, di * c - dr * s
            out[k] = (er + tr, ei + ti)
            out[n // 2 - k] = (er - tr, ti - ei)
    return out


def spread(source, target, first, at):
    for s in range(source.shape[0]):
        target[pl.ds(first * PITCH + s, source.shape[1], stride=PITCH), :] = source[s, :, at].astype(F32)


def butterflies(filt, low):
    def butterfly(b, _):
        at = pl.ds(pl.multiple_of(b * SBLK, SBLK), SBLK)
        for half in range(filt.shape[2] // LANES):
            to = slice(half * LANES, (half + 1) * LANES)
            parts = real_dft([filt[tile, at, to].astype(F32) for tile in range(RADIX)])
            for k, (re, im) in enumerate(parts):
                low[k, at, to] = re.astype(BF)
                if im is not None:
                    low[RADIX // 2 + k, at, to] = im.astype(BF)
        return 0

    lax.fori_loop(0, filt.shape[1] // SBLK, butterfly, 0)


def products(low, turned, pairs_ref, ends_ref):
    dests = ends_ref.shape[1] // 2
    pitch = 2 * RADIX + PAD

    def keep(channel, part, value):
        for tile in range(low.shape[1] // LANES):
            turned[tile, pl.ds(channel * 2 + part, dests, stride=pitch), :] = value[
                :, tile * LANES : (tile + 1) * LANES
            ]

    for end in range(2):
        z = lax.dot_general(
            ends_ref[end], low[end * (RADIX // 2)], NT, preferred_element_type=F32
        )
        for part in range(2):
            keep(end * (RADIX // 2), part, z[part * dests : (part + 1) * dests])

    def pair(k, _):
        spectrum = jnp.concatenate([low[k], low[RADIX // 2 + k]], axis=1)
        for mirrored in range(2):
            z = lax.dot_general(
                pairs_ref[k - 1, mirrored * 2 * dests : (mirrored + 1) * 2 * dests, :],
                spectrum,
                NT,
                preferred_element_type=F32,
            )
            channel = RADIX - k if mirrored else k
            for part in range(2):
                keep(channel, part, z[part * dests : (part + 1) * dests])
        return 0

    lax.fori_loop(1, RADIX // 2, pair, 0, unroll=RADIX // 2 - 1)


def own_kernel(
    keep_ref,
    x_hbm,
    taps_ref,
    pairs_hbm,
    ends_hbm,
    out_ref,
    part_ref,
    xs,
    filt,
    low,
    turned,
    x_ref,
    pairs_ref,
    ends_ref,
    sems,
):
    piece = x_hbm.shape[2] // PIECES
    samples = []
    for i in range(PIECES):
        part = (slice(None), slice(None), pl.ds(i * piece, piece))
        samples.append(pltpu.make_async_copy(x_hbm.at[part], x_ref.at[part], sems.at[2 + i]))
        samples[i].start()
    fetches = [
        pltpu.make_async_copy(pairs_hbm, pairs_ref, sems.at[0]),
        pltpu.make_async_copy(ends_hbm, ends_ref, sems.at[1]),
    ]
    for fetch in fetches:
        fetch.start()
    stations, frames, length = x_ref.shape
    taps = taps_ref.shape[0]
    span = length // RADIX
    own = keep_ref[0]
    done = range(HALO, 2 * HALO)

    def fir(tile, _):
        for half in range(span // LANES):
            at = pl.ds(pl.multiple_of(tile * span + half * LANES, LANES), LANES)
            spread(x_ref, xs, 0, at)
            weights = [taps_ref[pl.ds(k, 1), at] for k in range(taps)]
            sums = {}
            for step in range(frames):
                x = xs[step * PITCH : step * PITCH + stations, :]
                for k in range(taps - 1, -1, -1):
                    b = step + HALO - (taps - 1) + k
                    if 0 <= b < frames:
                        term = weights[k] * x
                        sums[b] = sums[b] + term if b in sums else term
                ready = [b for b in sums if b == step + HALO - (taps - 1) or step == frames - 1]
                for b in ready:
                    value = sums.pop(b)
                    if b in done:
                        place = b - done.start
                        to = slice(half * LANES, (half + 1) * LANES)
                        filt[tile, place * stations : (place + 1) * stations, to] = value.astype(BF)
                    else:
                        place = b if b < done.start else b - len(done)
                        if b + taps - 1 >= HALO + frames:
                            value = own * value
                        part_ref[2 * tile + half, place * stations : (place + 1) * stations, :] = value
        return 0

    for i in range(PIECES):
        samples[i].wait()
        lax.fori_loop(i * RADIX // PIECES, (i + 1) * RADIX // PIECES, fir, 0)
    butterflies(filt, low)
    for fetch in fetches:
        fetch.wait()
    products(low, turned, pairs_ref, ends_ref)

    def give(d, _):
        at = pl.ds(pl.multiple_of(d * (2 * RADIX + PAD), 8), 2 * RADIX)
        out_ref[d] = turned[0, at, :].astype(BF)
        return 0

    lax.fori_loop(0, out_ref.shape[0], give, 0, unroll=8)


def rest_kernel(
    left_ref, right_ref, taps_ref, pairs_ref, ends_ref, done_ref, part_ref, out_hbm, xs, filt, low, turned, stage, sems
):
    width = stage.shape[2]
    finished = pltpu.make_async_copy(done_ref, out_hbm.at[:, :, width:], sems.at[PIECES])
    finished.start()
    stations, _, length = left_ref.shape
    taps = taps_ref.shape[0]
    span = length // RADIX
    count = part_ref.shape[1] // stations

    def fir(tile, _):
        for half in range(span // LANES):
            at = pl.ds(pl.multiple_of(tile * span + half * LANES, LANES), LANES)
            lanes = slice(half * LANES, (half + 1) * LANES)
            spread(left_ref, xs, 0, at)
            spread(right_ref, xs, HALO, at)
            weights = [taps_ref[pl.ds(k, 1), at] for k in range(taps)]
            x = [xs[step * PITCH : step * PITCH + stations, :] for step in range(2 * HALO)]
            for place in range(count):
                to = slice(place * stations, (place + 1) * stations)
                value = part_ref[2 * tile + half, to, :]
                if place < HALO:
                    terms = [(j, taps - 1 - (j - place)) for j in range(place, HALO)]
                else:
                    first = place - (count - (HALO - 1))
                    terms = [(HALO + j, first - j) for j in range(first + 1)]
                for j, k in terms:
                    value = value + weights[k] * x[j]
                filt[tile, to, lanes] = value.astype(BF)
        return 0

    lax.fori_loop(0, RADIX, fir, 0)
    butterflies(filt, low)
    products(low, turned, pairs_ref, ends_ref)
    count = stage.shape[0] // PIECES
    copies = []
    for piece in range(PIECES):

        def give(d, _):
            at = pl.ds(pl.multiple_of(d * (2 * RADIX + PAD), 8), 2 * RADIX)
            for tile in range(width // LANES):
                stage[d, :, tile * LANES : (tile + 1) * LANES] = turned[tile, at, :].astype(BF)
            return 0

        lax.fori_loop(piece * count, (piece + 1) * count, give, 0, unroll=8)
        to = pl.ds(piece * count, count)
        copy = pltpu.make_async_copy(stage.at[to], out_hbm.at[to, :, :width], sems.at[piece])
        copy.start()
        copies.append(copy)
    for copy in copies + [finished]:
        copy.wait()


def channel_scratch(frames, steps, length):
    rows = frames * SBLK
    return [
        pltpu.VMEM(((steps + 1) * PITCH, LANES), F32),
        pltpu.VMEM((RADIX, rows, length // RADIX), BF),
        pltpu.VMEM((RADIX, rows, length // RADIX), BF),
        pltpu.VMEM((rows // LANES, (length // (2 * RADIX) + 1) * (2 * RADIX + PAD), LANES), F32),
    ]


def channelize_own(keep, samples, taps, pairs, ends):
    stations, frames, length = samples.shape
    dests = length // (2 * RADIX)
    whole = pl.BlockSpec(memory_space=pltpu.VMEM)
    return pl.pallas_call(
        own_kernel,
        out_shape=[
            jax.ShapeDtypeStruct((dests, 2 * RADIX, HALO * stations), BF),
            jax.ShapeDtypeStruct((length // LANES, (frames - HALO) * stations, LANES), F32),
        ],
        in_specs=[pl.BlockSpec(memory_space=pltpu.SMEM)]
        + [pl.BlockSpec(memory_space=pltpu.HBM), whole]
        + [pl.BlockSpec(memory_space=pltpu.HBM)] * 2,
        out_specs=[whole] * 2,
        scratch_shapes=channel_scratch(HALO, frames, length)
        + [
            pltpu.VMEM(samples.shape, BF),
            pltpu.VMEM(pairs.shape, BF),
            pltpu.VMEM(ends.shape, BF),
            pltpu.SemaphoreType.DMA((2 + PIECES,)),
        ],
        compiler_params=pltpu.CompilerParams(vmem_limit_bytes=22 << 20),
        cost_estimate=pl.CostEstimate(
            flops=10 * samples.size * 1000, bytes_accessed=20 << 20, transcendentals=0
        ),
        name="own",
    )(
        keep,
        pltpu.with_memory_space_constraint(samples, pltpu.HBM),
        taps,
        pltpu.with_memory_space_constraint(pairs, pltpu.HBM),
        pltpu.with_memory_space_constraint(ends, pltpu.HBM),
    )


def channelize_rest(before, after, taps, pairs, ends, done, part):
    stations, _, length = before.shape
    dests = length // (2 * RADIX)
    frames = part.shape[1] // stations
    whole = pl.BlockSpec(memory_space=pltpu.VMEM)
    return pl.pallas_call(
        rest_kernel,
        out_shape=jax.ShapeDtypeStruct((dests, 2 * RADIX, part.shape[1] + done.shape[2]), BF),
        in_specs=[whole] * 7,
        out_specs=pl.BlockSpec(memory_space=pltpu.HBM),
        scratch_shapes=channel_scratch(frames, 2 * HALO, length)
        + [
            pltpu.VMEM((dests, 2 * RADIX, part.shape[1]), BF),
            pltpu.SemaphoreType.DMA((PIECES + 1,)),
        ],
        compiler_params=pltpu.CompilerParams(vmem_limit_bytes=28 << 20),
        name="rest",
    )(before, after, taps, pairs, ends, done, part)


def swap_groups(v):
    group = lax.broadcasted_iota(jnp.int32, v[0].shape, 1) // SBLK
    v = [pltpu.roll(a, i * SBLK, 1) if i else a for i, a in enumerate(v)]
    v = [v[-i % 8] for i in range(8)]
    for bit in (1, 2, 4):
        odd = (group & bit) != 0
        v = [jnp.where(odd, v[(i - bit) % 8], v[i]) for i in range(8)]
    return [pltpu.roll(a, LANES - j * SBLK, 1) if j else a for j, a in enumerate(v)]


def weights_kernel(u_ref, v_ref, out_ref):
    cells = SBLK * SBLK
    for m in range(out_ref.shape[0]):
        u = u_ref[:, m * cells : (m + 1) * cells].astype(F32)
        v = v_ref[:, m * cells : (m + 1) * cells].astype(F32)
        cell_rows = jnp.concatenate([u[i : i + 1, :] * v for i in range(GRID)], axis=0)
        out_ref[m] = cell_rows.T.astype(BF)


def grid_weights(kern_u, kern_v):
    cells = SBLK * SBLK
    count = kern_u.shape[1] // cells
    step = math.gcd(count, 8)
    part = pl.BlockSpec((GRID, step * cells), lambda m: (0, m))
    return pl.pallas_call(
        weights_kernel,
        grid=(count // step,),
        out_shape=jax.ShapeDtypeStruct((count, cells, GRID * GRID), BF),
        in_specs=[part, part],
        out_specs=pl.BlockSpec((step, cells, GRID * GRID), lambda m: (m, 0, 0)),
        compiler_params=pltpu.CompilerParams(vmem_limit_bytes=16 << 20),
        cost_estimate=pl.CostEstimate(
            flops=count * GRID * GRID * cells, bytes_accessed=2 * count * GRID * GRID * cells, transcendentals=0
        ),
        name="grid_weights",
    )(kern_u, kern_v)


def correlate_kernel(sizes, slots_ref, r_ref, k_ref, out_ref, arr, vis, weights, acc, sem):
    owners, times, frames = sizes
    group2 = r_ref.shape[1]
    total = times * frames
    stations = owners * SBLK
    sides = stations // LANES
    arr_pitch = total + PAD
    vis_pitch = group2 + PAD
    fetch = pltpu.make_async_copy(k_ref, weights, sem)
    fetch.start()

    def turn(t, _):
        for tile in range(frames // 8):
            for side in range(sides):
                got = [
                    r_ref[(side * 8 + i) * times + t, :, tile * LANES : (tile + 1) * LANES]
                    for i in range(8)
                ]
                for i, w in enumerate(swap_groups(got)):
                    arr[side, pl.ds(t * frames + tile * 8 + i, group2, stride=arr_pitch), :] = w.astype(F32)
        return 0

    lax.fori_loop(0, times, turn, 0)

    def correlate(g, _):
        def part(side, c):
            at = pl.ds(pl.multiple_of((2 * g + c) * arr_pitch, 8), total)
            return arr[side, at, :].astype(BF)

        re = [part(side, 0) for side in range(sides)]
        im = [part(side, 1) for side in range(sides)]
        for side in range(sides):
            left = jnp.concatenate(
                [jnp.concatenate(re[: side + 1], axis=1), jnp.concatenate(im[: side + 1], axis=1)], axis=0
            )
            right = jnp.concatenate(
                [
                    jnp.concatenate([re[side], -im[side]], axis=1),
                    jnp.concatenate([im[side], re[side]], axis=1),
                ],
                axis=0,
            )
            z = lax.dot_general(left, right, TN, preferred_element_type=F32)
            for c in range(2):
                vis[side, pl.ds(2 * g + c, (side + 1) * LANES, stride=vis_pitch), :] = z[
                    :, c * LANES : (c + 1) * LANES
                ]
        return 0

    lax.fori_loop(0, group2 // 2, correlate, 0, unroll=8)

    acc[...] = jnp.zeros_like(acc)
    fetch.wait()

    m = 0
    for p in range(owners - 1):
        halves = {}
        for side in range(sides):
            if p >= side * 8 + 7:
                continue
            for half in range(2):
                got = [
                    vis[side, pl.ds((p * SBLK + half * 8 + i) * vis_pitch, group2), :].astype(BF)
                    for i in range(8)
                ]
                for i, w in enumerate(swap_groups(got)):
                    halves[side * 8 + i, half] = w
        for q in range(p + 1, owners):
            block = jnp.concatenate([halves[q, 0], halves[q, 1]], axis=1)
            z = jnp.dot(block, weights[m], preferred_element_type=F32)
            slot = slots_ref[m]
            acc[slot] = acc[slot] + z
            m += 1
    out_ref[...] = (acc[...] * (1.0 / math.sqrt(total))).astype(BF)


def correlate(turned, slots, weights, owners, times, frames, tiles):
    group2 = turned.shape[1]
    stations = owners * SBLK
    whole = pl.BlockSpec(memory_space=pltpu.VMEM)
    smem = pl.BlockSpec(memory_space=pltpu.SMEM)
    return pl.pallas_call(
        functools.partial(correlate_kernel, (owners, times, frames)),
        out_shape=jax.ShapeDtypeStruct((tiles, group2, GRID * GRID), BF),
        in_specs=[smem, whole, pl.BlockSpec(memory_space=pl.ANY)],
        out_specs=whole,
        scratch_shapes=[
            pltpu.VMEM((stations // LANES, (group2 + 1) * (times * frames + PAD), LANES), F32),
            pltpu.VMEM((stations // LANES, (stations + 1) * (group2 + PAD), LANES), F32),
            pltpu.VMEM(weights.shape, BF),
            pltpu.VMEM((tiles, group2, GRID * GRID), F32),
            pltpu.SemaphoreType.DMA,
        ],
        compiler_params=pltpu.CompilerParams(vmem_limit_bytes=42 << 20),
        name="correlate",
    )(slots, turned, weights)


def body(samples, taps, block_tile, tile_slots, kern_u, kern_v):
    frame_count = samples.shape[1]
    chan_size = lax.axis_size("chan")
    tm_size = lax.axis_size("tm")
    last, first = samples[:, frame_count - HALO :], samples[:, :HALO]
    before = lax.ppermute(last, "tm", [(i, i + 1) for i in range(tm_size - 1)])
    after = lax.ppermute(first, "tm", [((i + 1) % tm_size, i) for i in range(tm_size)])
    keep = (lax.axis_index("tm") < tm_size - 1).astype(F32).reshape(1)
    weights = grid_weights(kern_u, kern_v)
    pairs, ends = (jnp.asarray(table) for table in dft_tables(samples.shape[2]))
    done, part = channelize_own(keep, samples, taps, pairs, ends)
    spectra = channelize_rest(before, after, taps, pairs, ends, done, part)
    turned = lax.all_to_all(spectra, ("chan", "tm"), split_axis=0, concat_axis=0, tiled=True)
    tile_count = tile_slots.shape[0]
    slot_ids = jnp.arange(tile_count, dtype=jnp.int32)
    slots = jnp.sum(
        jnp.where(block_tile[:, None] == tile_slots[None, :], slot_ids[None, :], 0), axis=1
    )
    grids = correlate(turned, slots, weights, chan_size, tm_size, frame_count, tile_count)
    width = grids.shape[1] // 2
    partial_value = grids.reshape(tile_count, width, 2, GRID * GRID)
    return lax.all_to_all(partial_value, "tm", split_axis=0, concat_axis=1, tiled=True).astype(F32)


def solution(mesh):
    placed = (P("chan", "tm", None), P(), P(), P(), P(), P())
    return jax.shard_map(
        body, mesh=mesh, in_specs=placed, out_specs=P("tm", "chan", None, None), check_vma=False
    )
```

```python
import functools
import math

import jax
import jax.numpy as jnp
import ml_dtypes
import numpy as np
from jax import lax
from jax.experimental import pallas as pl
from jax.experimental.pallas import tpu as pltpu
from jax.sharding import PartitionSpec as P

SBLK = 16
GRID = 16
RADIX = 16
HALO = 8
PITCH = 24
PAD = 8
PIECES = 4
LANES = 128
BF = jnp.bfloat16
F32 = jnp.float32
NT = (((1,), (1,)), ((), ()))
TN = (((0,), (0,)), ((), ()))


def dft_tables(length):
    span = length // RADIX
    place = np.arange(span)[None, :]
    dest = np.arange(length // (2 * RADIX))[:, None]

    def table(low):
        angle = (place * (low + RADIX * dest) % length) * (2.0 * np.pi / length)
        c, s = np.cos(angle), np.sin(angle)
        sign = -1.0 if low > RADIX // 2 else 1.0
        return np.block([[c, sign * s], [-s, sign * c]]) / math.sqrt(length)

    pairs = np.stack(
        [np.concatenate([table(k), table(RADIX - k)], axis=0) for k in range(1, RADIX // 2)]
    )
    ends = np.stack([table(0)[:, :span], table(RADIX // 2)[:, :span]])
    return pairs.astype(ml_dtypes.bfloat16), ends.astype(ml_dtypes.bfloat16)


def real_dft(x):
    n = len(x)
    if n == 2:
        return [(x[0] + x[1], None), (x[0] - x[1], None)]
    even, odd = real_dft(x[0::2]), real_dft(x[1::2])
    out = [None] * (n // 2 + 1)
    for k in range(n // 4 + 1):
        er, ei = even[k]
        dr, di = odd[k]
        if k == 0:
            out[0], out[n // 2] = (er + dr, None), (er - dr, None)
        elif k == n // 4:
            out[k] = (er, -dr)
        else:
            c, s = math.cos(2 * math.pi * k / n), math.sin(2 * math.pi * k / n)
            if 8 * k == n:
                tr, ti = (dr + di) * c, (di - dr) * c
            else:
                tr, ti = dr * c + di * s, di * c - dr * s
            out[k] = (er + tr, ei + ti)
            out[n // 2 - k] = (er - tr, ti - ei)
    return out


def spread(source, target, first, at):
    for s in range(source.shape[0]):
        target[pl.ds(first * PITCH + s, source.shape[1], stride=PITCH), :] = source[s, :, at].astype(F32)


def butterflies(filt, low):
    def butterfly(b, _):
        at = pl.ds(pl.multiple_of(b * SBLK, SBLK), SBLK)
        for half in range(filt.shape[2] // LANES):
            to = slice(half * LANES, (half + 1) * LANES)
            parts = real_dft([filt[tile, at, to].astype(F32) for tile in range(RADIX)])
            for k, (re, im) in enumerate(parts):
                low[k, at, to] = re.astype(BF)
                if im is not None:
                    low[RADIX // 2 + k, at, to] = im.astype(BF)
        return 0

    lax.fori_loop(0, filt.shape[1] // SBLK, butterfly, 0)


def products(low, turned, pairs_ref, ends_ref):
    dests = ends_ref.shape[1] // 2
    pitch = 2 * RADIX + PAD

    def keep(channel, part, value):
        for tile in range(low.shape[1] // LANES):
            turned[tile, pl.ds(channel * 2 + part, dests, stride=pitch), :] = value[
                :, tile * LANES : (tile + 1) * LANES
            ]

    for end in range(2):
        z = lax.dot_general(
            ends_ref[end], low[end * (RADIX // 2)], NT, preferred_element_type=F32
        )
        for part in range(2):
            keep(end * (RADIX // 2), part, z[part * dests : (part + 1) * dests])

    def pair(k, _):
        spectrum = jnp.concatenate([low[k], low[RADIX // 2 + k]], axis=1)
        for mirrored in range(2):
            z = lax.dot_general(
                pairs_ref[k - 1, mirrored * 2 * dests : (mirrored + 1) * 2 * dests, :],
                spectrum,
                NT,
                preferred_element_type=F32,
            )
            channel = RADIX - k if mirrored else k
            for part in range(2):
                keep(channel, part, z[part * dests : (part + 1) * dests])
        return 0

    lax.fori_loop(1, RADIX // 2, pair, 0, unroll=RADIX // 2 - 1)


def own_kernel(
    keep_ref,
    x_hbm,
    taps_ref,
    pairs_hbm,
    ends_hbm,
    out_ref,
    part_ref,
    xs,
    filt,
    low,
    turned,
    x_ref,
    pairs_ref,
    ends_ref,
    sems,
):
    piece = x_hbm.shape[2] // PIECES
    samples = []
    for i in range(PIECES):
        part = (slice(None), slice(None), pl.ds(i * piece, piece))
        samples.append(pltpu.make_async_copy(x_hbm.at[part], x_ref.at[part], sems.at[2 + i]))
        samples[i].start()
    fetches = [
        pltpu.make_async_copy(pairs_hbm, pairs_ref, sems.at[0]),
        pltpu.make_async_copy(ends_hbm, ends_ref, sems.at[1]),
    ]
    for fetch in fetches:
        fetch.start()
    stations, frames, length = x_ref.shape
    taps = taps_ref.shape[0]
    span = length // RADIX
    own = keep_ref[0]
    done = range(HALO, 2 * HALO)

    def fir(tile, _):
        for half in range(span // LANES):
            at = pl.ds(pl.multiple_of(tile * span + half * LANES, LANES), LANES)
            spread(x_ref, xs, 0, at)
            weights = [taps_ref[pl.ds(k, 1), at] for k in range(taps)]
            sums = {}
            for step in range(frames):
                x = xs[step * PITCH : step * PITCH + stations, :]
                for k in range(taps - 1, -1, -1):
                    b = step + HALO - (taps - 1) + k
                    if 0 <= b < frames:
                        term = weights[k] * x
                        sums[b] = sums[b] + term if b in sums else term
                ready = [b for b in sums if b == step + HALO - (taps - 1) or step == frames - 1]
                for b in ready:
                    value = sums.pop(b)
                    if b in done:
                        place = b - done.start
                        to = slice(half * LANES, (half + 1) * LANES)
                        filt[tile, place * stations : (place + 1) * stations, to] = value.astype(BF)
                    else:
                        place = b if b < done.start else b - len(done)
                        if b + taps - 1 >= HALO + frames:
                            value = own * value
                        part_ref[2 * tile + half, place * stations : (place + 1) * stations, :] = value
        return 0

    for i in range(PIECES):
        samples[i].wait()
        lax.fori_loop(i * RADIX // PIECES, (i + 1) * RADIX // PIECES, fir, 0)
    butterflies(filt, low)
    for fetch in fetches:
        fetch.wait()
    products(low, turned, pairs_ref, ends_ref)

    def give(d, _):
        at = pl.ds(pl.multiple_of(d * (2 * RADIX + PAD), 8), 2 * RADIX)
        out_ref[d] = turned[0, at, :].astype(BF)
        return 0

    lax.fori_loop(0, out_ref.shape[0], give, 0, unroll=8)


def rest_kernel(
    right_ref, left_ref, taps_ref, pairs_ref, ends_ref, done_ref, part_ref, out_hbm, xs, filt, low, turned, stage, sems
):
    width = stage.shape[2]
    finished = pltpu.make_async_copy(done_ref, out_hbm.at[:, :, width:], sems.at[PIECES])
    finished.start()
    stations, _, length = left_ref.shape
    taps = taps_ref.shape[0]
    span = length // RADIX
    count = part_ref.shape[1] // stations

    def fir(tile, _):
        for half in range(span // LANES):
            at = pl.ds(pl.multiple_of(tile * span + half * LANES, LANES), LANES)
            lanes = slice(half * LANES, (half + 1) * LANES)
            spread(left_ref, xs, 0, at)
            spread(right_ref, xs, HALO, at)
            weights = [taps_ref[pl.ds(k, 1), at] for k in range(taps)]
            x = [xs[step * PITCH : step * PITCH + stations, :] for step in range(2 * HALO)]
            for place in range(count):
                to = slice(place * stations, (place + 1) * stations)
                value = part_ref[2 * tile + half, to, :]
                if place < HALO:
                    terms = [(j, taps - 1 - (j - place)) for j in range(place, HALO)]
                else:
                    first = place - (count - (HALO - 1))
                    terms = [(HALO + j, first - j) for j in range(first + 1)]
                for j, k in terms:
                    value = value + weights[k] * x[j]
                filt[tile, to, lanes] = value.astype(BF)
        return 0

    lax.fori_loop(0, RADIX, fir, 0)
    butterflies(filt, low)
    products(low, turned, pairs_ref, ends_ref)
    count = stage.shape[0] // PIECES
    copies = []
    for piece in range(PIECES):

        def give(d, _):
            at = pl.ds(pl.multiple_of(d * (2 * RADIX + PAD), 8), 2 * RADIX)
            for tile in range(width // LANES):
                stage[d, :, tile * LANES : (tile + 1) * LANES] = turned[tile, at, :].astype(BF)
            return 0

        lax.fori_loop(piece * count, (piece + 1) * count, give, 0, unroll=8)
        to = pl.ds(piece * count, count)
        copy = pltpu.make_async_copy(stage.at[to], out_hbm.at[to, :, :width], sems.at[piece])
        copy.start()
        copies.append(copy)
    for copy in copies + [finished]:
        copy.wait()


def channel_scratch(frames, steps, length):
    rows = frames * SBLK
    return [
        pltpu.VMEM(((steps + 1) * PITCH, LANES), F32),
        pltpu.VMEM((RADIX, rows, length // RADIX), BF),
        pltpu.VMEM((RADIX, rows, length // RADIX), BF),
        pltpu.VMEM((rows // LANES, (length // (2 * RADIX) + 1) * (2 * RADIX + PAD), LANES), F32),
    ]


def ends_kernel(x_ref, first_ref, last_ref, sems):
    frames = x_ref.shape[1]
    copies = [
        pltpu.make_async_copy(x_ref.at[:, :HALO, :], first_ref, sems.at[0]),
        pltpu.make_async_copy(x_ref.at[:, frames - HALO :, :], last_ref, sems.at[1]),
    ]
    for copy in copies:
        copy.start()
    for copy in copies:
        copy.wait()


def end_frames(samples):
    stations, _, length = samples.shape
    return pl.pallas_call(
        ends_kernel,
        out_shape=[jax.ShapeDtypeStruct((stations, HALO, length), BF)] * 2,
        in_specs=[pl.BlockSpec(memory_space=pltpu.HBM)],
        out_specs=[pl.BlockSpec(memory_space=pltpu.VMEM)] * 2,
        scratch_shapes=[pltpu.SemaphoreType.DMA((2,))],
        compiler_params=pltpu.CompilerParams(vmem_limit_bytes=8 << 20),
        name="end_frames",
    )(pltpu.with_memory_space_constraint(samples, pltpu.HBM))


def channelize_own(keep, samples, taps, pairs, ends):
    stations, frames, length = samples.shape
    dests = length // (2 * RADIX)
    whole = pl.BlockSpec(memory_space=pltpu.VMEM)
    return pl.pallas_call(
        own_kernel,
        out_shape=[
            jax.ShapeDtypeStruct((dests, 2 * RADIX, HALO * stations), BF),
            jax.ShapeDtypeStruct((length // LANES, (frames - HALO) * stations, LANES), F32),
        ],
        in_specs=[pl.BlockSpec(memory_space=pltpu.SMEM)]
        + [pl.BlockSpec(memory_space=pltpu.HBM), whole]
        + [pl.BlockSpec(memory_space=pltpu.HBM)] * 2,
        out_specs=[whole] * 2,
        scratch_shapes=channel_scratch(HALO, frames, length)
        + [
            pltpu.VMEM(samples.shape, BF),
            pltpu.VMEM(pairs.shape, BF),
            pltpu.VMEM(ends.shape, BF),
            pltpu.SemaphoreType.DMA((2 + PIECES,)),
        ],
        compiler_params=pltpu.CompilerParams(vmem_limit_bytes=22 << 20),
        cost_estimate=pl.CostEstimate(
            flops=10 * samples.size * 1000, bytes_accessed=20 << 20, transcendentals=0
        ),
        name="own",
    )(
        keep,
        pltpu.with_memory_space_constraint(samples, pltpu.HBM),
        taps,
        pltpu.with_memory_space_constraint(pairs, pltpu.HBM),
        pltpu.with_memory_space_constraint(ends, pltpu.HBM),
    )


def channelize_rest(before, after, taps, pairs, ends, done, part):
    stations, _, length = before.shape
    dests = length // (2 * RADIX)
    frames = part.shape[1] // stations
    whole = pl.BlockSpec(memory_space=pltpu.VMEM)
    return pl.pallas_call(
        rest_kernel,
        out_shape=jax.ShapeDtypeStruct((dests, 2 * RADIX, part.shape[1] + done.shape[2]), BF),
        in_specs=[whole] * 7,
        out_specs=pl.BlockSpec(memory_space=pltpu.HBM),
        scratch_shapes=channel_scratch(frames, 2 * HALO, length)
        + [
            pltpu.VMEM((dests, 2 * RADIX, part.shape[1]), BF),
            pltpu.SemaphoreType.DMA((PIECES + 1,)),
        ],
        compiler_params=pltpu.CompilerParams(vmem_limit_bytes=28 << 20),
        name="rest",
    )(after, before, taps, pairs, ends, done, part)


def swap_groups(v):
    group = lax.broadcasted_iota(jnp.int32, v[0].shape, 1) // SBLK
    v = [pltpu.roll(a, i * SBLK, 1) if i else a for i, a in enumerate(v)]
    v = [v[-i % 8] for i in range(8)]
    for bit in (1, 2, 4):
        odd = (group & bit) != 0
        v = [jnp.where(odd, v[(i - bit) % 8], v[i]) for i in range(8)]
    return [pltpu.roll(a, LANES - j * SBLK, 1) if j else a for j, a in enumerate(v)]


def weights_kernel(u_ref, v_ref, out_ref):
    cells = SBLK * SBLK
    for m in range(out_ref.shape[0]):
        u = u_ref[:, m * cells : (m + 1) * cells].astype(F32)
        v = v_ref[:, m * cells : (m + 1) * cells].astype(F32)
        cell_rows = jnp.concatenate([u[i : i + 1, :] * v for i in range(GRID)], axis=0)
        out_ref[m] = cell_rows.T.astype(BF)


def grid_weights(kern_u, kern_v):
    cells = SBLK * SBLK
    count = kern_u.shape[1] // cells
    step = math.gcd(count, 8)
    part = pl.BlockSpec((GRID, step * cells), lambda m: (0, m))
    return pl.pallas_call(
        weights_kernel,
        grid=(count // step,),
        out_shape=jax.ShapeDtypeStruct((count, cells, GRID * GRID), BF),
        in_specs=[part, part],
        out_specs=pl.BlockSpec((step, cells, GRID * GRID), lambda m: (m, 0, 0)),
        compiler_params=pltpu.CompilerParams(vmem_limit_bytes=16 << 20),
        cost_estimate=pl.CostEstimate(
            flops=count * GRID * GRID * cells, bytes_accessed=2 * count * GRID * GRID * cells, transcendentals=0
        ),
        name="grid_weights",
    )(kern_u, kern_v)


def correlate_kernel(sizes, slots_ref, r_ref, k_ref, out_ref, arr, vis, weights, acc, sem):
    owners, times, frames = sizes
    group2 = r_ref.shape[1]
    total = times * frames
    stations = owners * SBLK
    sides = stations // LANES
    arr_pitch = total + PAD
    vis_pitch = group2 + PAD
    fetch = pltpu.make_async_copy(k_ref, weights, sem)
    fetch.start()

    def turn(t, _):
        for tile in range(frames // 8):
            for side in range(sides):
                got = [
                    r_ref[(side * 8 + i) * times + t, :, tile * LANES : (tile + 1) * LANES]
                    for i in range(8)
                ]
                for i, w in enumerate(swap_groups(got)):
                    arr[side, pl.ds(t * frames + tile * 8 + i, group2, stride=arr_pitch), :] = w.astype(F32)
        return 0

    lax.fori_loop(0, times, turn, 0)

    def correlate(g, _):
        def part(side, c):
            at = pl.ds(pl.multiple_of((2 * g + c) * arr_pitch, 8), total)
            return arr[side, at, :].astype(BF)

        re = [part(side, 0) for side in range(sides)]
        im = [part(side, 1) for side in range(sides)]
        for side in range(sides):
            left = jnp.concatenate(
                [jnp.concatenate(re[: side + 1], axis=1), jnp.concatenate(im[: side + 1], axis=1)], axis=0
            )
            right = jnp.concatenate(
                [
                    jnp.concatenate([re[side], -im[side]], axis=1),
                    jnp.concatenate([im[side], re[side]], axis=1),
                ],
                axis=0,
            )
            z = lax.dot_general(left, right, TN, preferred_element_type=F32)
            for c in range(2):
                vis[side, pl.ds(2 * g + c, (side + 1) * LANES, stride=vis_pitch), :] = z[
                    :, c * LANES : (c + 1) * LANES
                ]
        return 0

    lax.fori_loop(0, group2 // 2, correlate, 0, unroll=8)

    acc[...] = jnp.zeros_like(acc)
    fetch.wait()

    m = 0
    for p in range(owners - 1):
        halves = {}
        for side in range(sides):
            if p >= side * 8 + 7:
                continue
            for half in range(2):
                got = [
                    vis[side, pl.ds((p * SBLK + half * 8 + i) * vis_pitch, group2), :].astype(BF)
                    for i in range(8)
                ]
                for i, w in enumerate(swap_groups(got)):
                    halves[side * 8 + i, half] = w
        for q in range(p + 1, owners):
            block = jnp.concatenate([halves[q, 0], halves[q, 1]], axis=1)
            z = jnp.dot(block, weights[m], preferred_element_type=F32)
            slot = slots_ref[m]
            acc[slot] = acc[slot] + z
            m += 1
    out_ref[...] = (acc[...] * (1.0 / math.sqrt(total))).astype(BF)


def correlate(turned, slots, weights, owners, times, frames, tiles):
    group2 = turned.shape[1]
    stations = owners * SBLK
    whole = pl.BlockSpec(memory_space=pltpu.VMEM)
    smem = pl.BlockSpec(memory_space=pltpu.SMEM)
    return pl.pallas_call(
        functools.partial(correlate_kernel, (owners, times, frames)),
        out_shape=jax.ShapeDtypeStruct((tiles, group2, GRID * GRID), BF),
        in_specs=[smem, whole, pl.BlockSpec(memory_space=pl.ANY)],
        out_specs=whole,
        scratch_shapes=[
            pltpu.VMEM((stations // LANES, (group2 + 1) * (times * frames + PAD), LANES), F32),
            pltpu.VMEM((stations // LANES, (stations + 1) * (group2 + PAD), LANES), F32),
            pltpu.VMEM(weights.shape, BF),
            pltpu.VMEM((tiles, group2, GRID * GRID), F32),
            pltpu.SemaphoreType.DMA,
        ],
        compiler_params=pltpu.CompilerParams(vmem_limit_bytes=42 << 20),
        name="correlate",
    )(slots, turned, weights)


def body(samples, taps, block_tile, tile_slots, kern_u, kern_v):
    frame_count = samples.shape[1]
    chan_size = lax.axis_size("chan")
    tm_size = lax.axis_size("tm")
    last, first = samples[:, frame_count - HALO :], samples[:, :HALO]
    first, last = end_frames(samples)
    after = lax.ppermute(first, "tm", [((i + 1) % tm_size, i) for i in range(tm_size)])
    before = lax.ppermute(last, "tm", [(i, i + 1) for i in range(tm_size - 1)])
    keep = (lax.axis_index("tm") < tm_size - 1).astype(F32).reshape(1)
    weights = grid_weights(kern_u, kern_v)
    pairs, ends = (jnp.asarray(table) for table in dft_tables(samples.shape[2]))
    done, part = channelize_own(keep, samples, taps, pairs, ends)
    spectra = channelize_rest(before, after, taps, pairs, ends, done, part)
    turned = lax.all_to_all(spectra, ("chan", "tm"), split_axis=0, concat_axis=0, tiled=True)
    tile_count = tile_slots.shape[0]
    slot_ids = jnp.arange(tile_count, dtype=jnp.int32)
    slots = jnp.sum(
        jnp.where(block_tile[:, None] == tile_slots[None, :], slot_ids[None, :], 0), axis=1
    )
    grids = correlate(turned, slots, weights, chan_size, tm_size, frame_count, tile_count)
    width = grids.shape[1] // 2
    partial_value = grids.reshape(tile_count, width, 2, GRID * GRID)
    return lax.all_to_all(partial_value, "tm", split_axis=0, concat_axis=1, tiled=True).astype(F32)


def solution(mesh):
    placed = (P("chan", "tm", None), P(), P(), P(), P(), P())
    return jax.shard_map(
        body, mesh=mesh, in_specs=placed, out_specs=P("tm", "chan", None, None), check_vma=False
    )
```

```python
import functools
import math

import jax
import jax.numpy as jnp
import ml_dtypes
import numpy as np
from jax import lax
from jax.experimental import pallas as pl
from jax.experimental.pallas import tpu as pltpu
from jax.sharding import PartitionSpec as P

SBLK = 16
GRID = 16
RADIX = 16
HALO = 8
PITCH = 24
PAD = 8
PIECES = 4
LANES = 128
BF = jnp.bfloat16
F32 = jnp.float32
NT = (((1,), (1,)), ((), ()))
TN = (((0,), (0,)), ((), ()))


def dft_tables(length):
    span = length // RADIX
    place = np.arange(span)[None, :]
    dest = np.arange(length // (2 * RADIX))[:, None]

    def table(low):
        angle = (place * (low + RADIX * dest) % length) * (2.0 * np.pi / length)
        c, s = np.cos(angle), np.sin(angle)
        sign = -1.0 if low > RADIX // 2 else 1.0
        return np.block([[c, sign * s], [-s, sign * c]]) / math.sqrt(length)

    pairs = np.stack(
        [np.concatenate([table(k), table(RADIX - k)], axis=0) for k in range(1, RADIX // 2)]
    )
    ends = np.stack([table(0)[:, :span], table(RADIX // 2)[:, :span]])
    return pairs.astype(ml_dtypes.bfloat16), ends.astype(ml_dtypes.bfloat16)


def real_dft(x):
    n = len(x)
    if n == 2:
        return [(x[0] + x[1], None), (x[0] - x[1], None)]
    even, odd = real_dft(x[0::2]), real_dft(x[1::2])
    out = [None] * (n // 2 + 1)
    for k in range(n // 4 + 1):
        er, ei = even[k]
        dr, di = odd[k]
        if k == 0:
            out[0], out[n // 2] = (er + dr, None), (er - dr, None)
        elif k == n // 4:
            out[k] = (er, -dr)
        else:
            c, s = math.cos(2 * math.pi * k / n), math.sin(2 * math.pi * k / n)
            if 8 * k == n:
                tr, ti = (dr + di) * c, (di - dr) * c
            else:
                tr, ti = dr * c + di * s, di * c - dr * s
            out[k] = (er + tr, ei + ti)
            out[n // 2 - k] = (er - tr, ti - ei)
    return out


def spread(source, target, first, at):
    for s in range(source.shape[0]):
        target[pl.ds(first * PITCH + s, source.shape[1], stride=PITCH), :] = source[s, :, at].astype(F32)


def butterflies(filt, low):
    def butterfly(b, _):
        at = pl.ds(pl.multiple_of(b * SBLK, SBLK), SBLK)
        for half in range(filt.shape[2] // LANES):
            to = slice(half * LANES, (half + 1) * LANES)
            parts = real_dft([filt[tile, at, to].astype(F32) for tile in range(RADIX)])
            for k, (re, im) in enumerate(parts):
                low[k, at, to] = re.astype(BF)
                if im is not None:
                    low[RADIX // 2 + k, at, to] = im.astype(BF)
        return 0

    lax.fori_loop(0, filt.shape[1] // SBLK, butterfly, 0)


def products(low, turned, pairs_ref, ends_ref):
    dests = ends_ref.shape[1] // 2
    pitch = 2 * RADIX + PAD

    def keep(channel, part, value):
        for tile in range(low.shape[1] // LANES):
            turned[tile, pl.ds(channel * 2 + part, dests, stride=pitch), :] = value[
                :, tile * LANES : (tile + 1) * LANES
            ]

    for end in range(2):
        z = lax.dot_general(
            ends_ref[end], low[end * (RADIX // 2)], NT, preferred_element_type=F32
        )
        for part in range(2):
            keep(end * (RADIX // 2), part, z[part * dests : (part + 1) * dests])

    def pair(k, _):
        spectrum = jnp.concatenate([low[k], low[RADIX // 2 + k]], axis=1)
        for mirrored in range(2):
            z = lax.dot_general(
                pairs_ref[k - 1, mirrored * 2 * dests : (mirrored + 1) * 2 * dests, :],
                spectrum,
                NT,
                preferred_element_type=F32,
            )
            channel = RADIX - k if mirrored else k
            for part in range(2):
                keep(channel, part, z[part * dests : (part + 1) * dests])
        return 0

    lax.fori_loop(1, RADIX // 2, pair, 0, unroll=RADIX // 2 - 1)


def own_kernel(
    keep_ref,
    x_hbm,
    taps_ref,
    pairs_hbm,
    ends_hbm,
    out_ref,
    part_ref,
    xs,
    filt,
    low,
    turned,
    x_ref,
    pairs_ref,
    ends_ref,
    sems,
):
    piece = x_hbm.shape[2] // PIECES
    samples = []
    for i in range(PIECES):
        part = (slice(None), slice(None), pl.ds(i * piece, piece))
        samples.append(pltpu.make_async_copy(x_hbm.at[part], x_ref.at[part], sems.at[2 + i]))
        samples[i].start()
    fetches = [
        pltpu.make_async_copy(pairs_hbm, pairs_ref, sems.at[0]),
        pltpu.make_async_copy(ends_hbm, ends_ref, sems.at[1]),
    ]
    for fetch in fetches:
        fetch.start()
    stations, frames, length = x_ref.shape
    taps = taps_ref.shape[0]
    span = length // RADIX
    own = keep_ref[0]
    done = range(HALO, 2 * HALO)

    def fir(tile, _):
        for half in range(span // LANES):
            at = pl.ds(pl.multiple_of(tile * span + half * LANES, LANES), LANES)
            spread(x_ref, xs, 0, at)
            weights = [taps_ref[pl.ds(k, 1), at] for k in range(taps)]
            sums = {}
            for step in range(frames):
                x = xs[step * PITCH : step * PITCH + stations, :]
                for k in range(taps - 1, -1, -1):
                    b = step + HALO - (taps - 1) + k
                    if 0 <= b < frames:
                        term = weights[k] * x
                        sums[b] = sums[b] + term if b in sums else term
                ready = [b for b in sums if b == step + HALO - (taps - 1) or step == frames - 1]
                for b in ready:
                    value = sums.pop(b)
                    if b in done:
                        place = b - done.start
                        to = slice(half * LANES, (half + 1) * LANES)
                        filt[tile, place * stations : (place + 1) * stations, to] = value.astype(BF)
                    else:
                        place = b if b < done.start else b - len(done)
                        if b + taps - 1 >= HALO + frames:
                            value = own * value
                        part_ref[2 * tile + half, place * stations : (place + 1) * stations, :] = value
        return 0

    for i in range(PIECES):
        samples[i].wait()
        lax.fori_loop(i * RADIX // PIECES, (i + 1) * RADIX // PIECES, fir, 0)
    butterflies(filt, low)
    for fetch in fetches:
        fetch.wait()
    products(low, turned, pairs_ref, ends_ref)

    def give(d, _):
        at = pl.ds(pl.multiple_of(d * (2 * RADIX + PAD), 8), 2 * RADIX)
        out_ref[d] = turned[0, at, :].astype(BF)
        return 0

    lax.fori_loop(0, out_ref.shape[0], give, 0, unroll=8)


def rest_kernel(
    right_ref, left_ref, taps_ref, pairs_ref, ends_ref, done_ref, part_ref, out_hbm, xs, filt, low, turned, stage, sems
):
    width = stage.shape[2]
    finished = pltpu.make_async_copy(done_ref, out_hbm.at[:, :, width:], sems.at[PIECES])
    finished.start()
    stations, _, length = left_ref.shape
    taps = taps_ref.shape[0]
    span = length // RADIX
    count = part_ref.shape[1] // stations

    def fir(tile, _):
        for half in range(span // LANES):
            at = pl.ds(pl.multiple_of(tile * span + half * LANES, LANES), LANES)
            lanes = slice(half * LANES, (half + 1) * LANES)
            spread(left_ref, xs, 0, at)
            spread(right_ref, xs, HALO, at)
            weights = [taps_ref[pl.ds(k, 1), at] for k in range(taps)]
            x = [xs[step * PITCH : step * PITCH + stations, :] for step in range(2 * HALO)]
            for place in range(count):
                to = slice(place * stations, (place + 1) * stations)
                value = part_ref[2 * tile + half, to, :]
                if place < HALO:
                    terms = [(j, taps - 1 - (j - place)) for j in range(place, HALO)]
                else:
                    first = place - (count - (HALO - 1))
                    terms = [(HALO + j, first - j) for j in range(first + 1)]
                for j, k in terms:
                    value = value + weights[k] * x[j]
                filt[tile, to, lanes] = value.astype(BF)
        return 0

    lax.fori_loop(0, RADIX, fir, 0, unroll=2)
    butterflies(filt, low)
    products(low, turned, pairs_ref, ends_ref)
    count = stage.shape[0] // PIECES
    copies = []
    for piece in range(PIECES):

        def give(d, _):
            at = pl.ds(pl.multiple_of(d * (2 * RADIX + PAD), 8), 2 * RADIX)
            for tile in range(width // LANES):
                stage[d, :, tile * LANES : (tile + 1) * LANES] = turned[tile, at, :].astype(BF)
            return 0

        lax.fori_loop(piece * count, (piece + 1) * count, give, 0, unroll=8)
        to = pl.ds(piece * count, count)
        copy = pltpu.make_async_copy(stage.at[to], out_hbm.at[to, :, :width], sems.at[piece])
        copy.start()
        copies.append(copy)
    for copy in copies + [finished]:
        copy.wait()


def channel_scratch(frames, steps, length):
    rows = frames * SBLK
    return [
        pltpu.VMEM(((steps + 1) * PITCH, LANES), F32),
        pltpu.VMEM((RADIX, rows, length // RADIX), BF),
        pltpu.VMEM((RADIX, rows, length // RADIX), BF),
        pltpu.VMEM((rows // LANES, (length // (2 * RADIX) + 1) * (2 * RADIX + PAD), LANES), F32),
    ]


def ends_kernel(x_ref, first_ref, last_ref, sems):
    frames = x_ref.shape[1]
    copies = [
        pltpu.make_async_copy(x_ref.at[:, :HALO, :], first_ref, sems.at[0]),
        pltpu.make_async_copy(x_ref.at[:, frames - HALO :, :], last_ref, sems.at[1]),
    ]
    for copy in copies:
        copy.start()
    for copy in copies:
        copy.wait()


def end_frames(samples):
    stations, _, length = samples.shape
    return pl.pallas_call(
        ends_kernel,
        out_shape=[jax.ShapeDtypeStruct((stations, HALO, length), BF)] * 2,
        in_specs=[pl.BlockSpec(memory_space=pltpu.HBM)],
        out_specs=[pl.BlockSpec(memory_space=pltpu.VMEM)] * 2,
        scratch_shapes=[pltpu.SemaphoreType.DMA((2,))],
        compiler_params=pltpu.CompilerParams(vmem_limit_bytes=8 << 20),
        name="end_frames",
    )(pltpu.with_memory_space_constraint(samples, pltpu.HBM))


def channelize_own(keep, samples, taps, pairs, ends):
    stations, frames, length = samples.shape
    dests = length // (2 * RADIX)
    whole = pl.BlockSpec(memory_space=pltpu.VMEM)
    return pl.pallas_call(
        own_kernel,
        out_shape=[
            jax.ShapeDtypeStruct((dests, 2 * RADIX, HALO * stations), BF),
            jax.ShapeDtypeStruct((length // LANES, (frames - HALO) * stations, LANES), F32),
        ],
        in_specs=[pl.BlockSpec(memory_space=pltpu.SMEM)]
        + [pl.BlockSpec(memory_space=pltpu.HBM), whole]
        + [pl.BlockSpec(memory_space=pltpu.HBM)] * 2,
        out_specs=[whole] * 2,
        scratch_shapes=channel_scratch(HALO, frames, length)
        + [
            pltpu.VMEM(samples.shape, BF),
            pltpu.VMEM(pairs.shape, BF),
            pltpu.VMEM(ends.shape, BF),
            pltpu.SemaphoreType.DMA((2 + PIECES,)),
        ],
        compiler_params=pltpu.CompilerParams(vmem_limit_bytes=22 << 20),
        cost_estimate=pl.CostEstimate(
            flops=10 * samples.size * 1000, bytes_accessed=20 << 20, transcendentals=0
        ),
        name="own",
    )(
        keep,
        pltpu.with_memory_space_constraint(samples, pltpu.HBM),
        taps,
        pltpu.with_memory_space_constraint(pairs, pltpu.HBM),
        pltpu.with_memory_space_constraint(ends, pltpu.HBM),
    )


def channelize_rest(before, after, taps, pairs, ends, done, part):
    stations, _, length = before.shape
    dests = length // (2 * RADIX)
    frames = part.shape[1] // stations
    whole = pl.BlockSpec(memory_space=pltpu.VMEM)
    return pl.pallas_call(
        rest_kernel,
        out_shape=jax.ShapeDtypeStruct((dests, 2 * RADIX, part.shape[1] + done.shape[2]), BF),
        in_specs=[whole] * 7,
        out_specs=pl.BlockSpec(memory_space=pltpu.HBM),
        scratch_shapes=channel_scratch(frames, 2 * HALO, length)
        + [
            pltpu.VMEM((dests, 2 * RADIX, part.shape[1]), BF),
            pltpu.SemaphoreType.DMA((PIECES + 1,)),
        ],
        compiler_params=pltpu.CompilerParams(vmem_limit_bytes=28 << 20),
        name="rest",
    )(after, before, taps, pairs, ends, done, part)


def swap_groups(v):
    group = lax.broadcasted_iota(jnp.int32, v[0].shape, 1) // SBLK
    v = [pltpu.roll(a, i * SBLK, 1) if i else a for i, a in enumerate(v)]
    v = [v[-i % 8] for i in range(8)]
    for bit in (1, 2, 4):
        odd = (group & bit) != 0
        v = [jnp.where(odd, v[(i - bit) % 8], v[i]) for i in range(8)]
    return [pltpu.roll(a, LANES - j * SBLK, 1) if j else a for j, a in enumerate(v)]


def weights_kernel(u_ref, v_ref, out_ref):
    cells = SBLK * SBLK
    for m in range(out_ref.shape[0]):
        u = u_ref[:, m * cells : (m + 1) * cells].astype(F32)
        v = v_ref[:, m * cells : (m + 1) * cells].astype(F32)
        cell_rows = jnp.concatenate([u[i : i + 1, :] * v for i in range(GRID)], axis=0)
        out_ref[m] = cell_rows.T.astype(BF)


def grid_weights(kern_u, kern_v):
    cells = SBLK * SBLK
    count = kern_u.shape[1] // cells
    step = math.gcd(count, 8)
    part = pl.BlockSpec((GRID, step * cells), lambda m: (0, m))
    return pl.pallas_call(
        weights_kernel,
        grid=(count // step,),
        out_shape=jax.ShapeDtypeStruct((count, cells, GRID * GRID), BF),
        in_specs=[part, part],
        out_specs=pl.BlockSpec((step, cells, GRID * GRID), lambda m: (m, 0, 0)),
        compiler_params=pltpu.CompilerParams(vmem_limit_bytes=16 << 20),
        cost_estimate=pl.CostEstimate(
            flops=count * GRID * GRID * cells, bytes_accessed=2 * count * GRID * GRID * cells, transcendentals=0
        ),
        name="grid_weights",
    )(kern_u, kern_v)


def correlate_kernel(sizes, slots_ref, r_ref, k_ref, out_ref, arr, vis, weights, acc, sem):
    owners, times, frames = sizes
    group2 = r_ref.shape[1]
    total = times * frames
    stations = owners * SBLK
    sides = stations // LANES
    arr_pitch = total + PAD
    vis_pitch = group2 + PAD
    fetch = pltpu.make_async_copy(k_ref, weights, sem)
    fetch.start()

    def turn(t, _):
        for tile in range(frames // 8):
            for side in range(sides):
                got = [
                    r_ref[(side * 8 + i) * times + t, :, tile * LANES : (tile + 1) * LANES]
                    for i in range(8)
                ]
                for i, w in enumerate(swap_groups(got)):
                    arr[side, pl.ds(t * frames + tile * 8 + i, group2, stride=arr_pitch), :] = w.astype(F32)
        return 0

    lax.fori_loop(0, times, turn, 0)

    def correlate(g, _):
        def part(side, c):
            at = pl.ds(pl.multiple_of((2 * g + c) * arr_pitch, 8), total)
            return arr[side, at, :].astype(BF)

        re = [part(side, 0) for side in range(sides)]
        im = [part(side, 1) for side in range(sides)]
        for side in range(sides):
            left = jnp.concatenate(
                [jnp.concatenate(re[: side + 1], axis=1), jnp.concatenate(im[: side + 1], axis=1)], axis=0
            )
            right = jnp.concatenate(
                [
                    jnp.concatenate([re[side], -im[side]], axis=1),
                    jnp.concatenate([im[side], re[side]], axis=1),
                ],
                axis=0,
            )
            z = lax.dot_general(left, right, TN, preferred_element_type=F32)
            for c in range(2):
                vis[side, pl.ds(2 * g + c, (side + 1) * LANES, stride=vis_pitch), :] = z[
                    :, c * LANES : (c + 1) * LANES
                ]
        return 0

    lax.fori_loop(0, group2 // 2, correlate, 0, unroll=8)

    acc[...] = jnp.zeros_like(acc)
    fetch.wait()

    m = 0
    for p in range(owners - 1):
        halves = {}
        for side in range(sides):
            if p >= side * 8 + 7:
                continue
            for half in range(2):
                got = [
                    vis[side, pl.ds((p * SBLK + half * 8 + i) * vis_pitch, group2), :].astype(BF)
                    for i in range(8)
                ]
                for i, w in enumerate(swap_groups(got)):
                    halves[side * 8 + i, half] = w
        for q in range(p + 1, owners):
            block = jnp.concatenate([halves[q, 0], halves[q, 1]], axis=1)
            z = jnp.dot(block, weights[m], preferred_element_type=F32)
            slot = slots_ref[m]
            acc[slot] = acc[slot] + z
            m += 1
    out_ref[...] = (acc[...] * (1.0 / math.sqrt(total))).astype(BF)


def correlate(turned, slots, weights, owners, times, frames, tiles):
    group2 = turned.shape[1]
    stations = owners * SBLK
    whole = pl.BlockSpec(memory_space=pltpu.VMEM)
    smem = pl.BlockSpec(memory_space=pltpu.SMEM)
    return pl.pallas_call(
        functools.partial(correlate_kernel, (owners, times, frames)),
        out_shape=jax.ShapeDtypeStruct((tiles, group2, GRID * GRID), BF),
        in_specs=[smem, whole, pl.BlockSpec(memory_space=pl.ANY)],
        out_specs=whole,
        scratch_shapes=[
            pltpu.VMEM((stations // LANES, (group2 + 1) * (times * frames + PAD), LANES), F32),
            pltpu.VMEM((stations // LANES, (stations + 1) * (group2 + PAD), LANES), F32),
            pltpu.VMEM(weights.shape, BF),
            pltpu.VMEM((tiles, group2, GRID * GRID), F32),
            pltpu.SemaphoreType.DMA,
        ],
        compiler_params=pltpu.CompilerParams(vmem_limit_bytes=42 << 20),
        name="correlate",
    )(slots, turned, weights)


def body(samples, taps, block_tile, tile_slots, kern_u, kern_v):
    frame_count = samples.shape[1]
    chan_size = lax.axis_size("chan")
    tm_size = lax.axis_size("tm")
    last, first = samples[:, frame_count - HALO :], samples[:, :HALO]
    first, last = end_frames(samples)
    after = lax.ppermute(first, "tm", [((i + 1) % tm_size, i) for i in range(tm_size)])
    before = lax.ppermute(last, "tm", [(i, i + 1) for i in range(tm_size - 1)])
    keep = (lax.axis_index("tm") < tm_size - 1).astype(F32).reshape(1)
    weights = grid_weights(kern_u, kern_v)
    pairs, ends = (jnp.asarray(table) for table in dft_tables(samples.shape[2]))
    done, part = channelize_own(keep, samples, taps, pairs, ends)
    spectra = channelize_rest(before, after, taps, pairs, ends, done, part)
    turned = lax.all_to_all(spectra, ("chan", "tm"), split_axis=0, concat_axis=0, tiled=True)
    tile_count = tile_slots.shape[0]
    slot_ids = jnp.arange(tile_count, dtype=jnp.int32)
    slots = jnp.sum(
        jnp.where(block_tile[:, None] == tile_slots[None, :], slot_ids[None, :], 0), axis=1
    )
    grids = correlate(turned, slots, weights, chan_size, tm_size, frame_count, tile_count)
    width = grids.shape[1] // 2
    partial_value = grids.reshape(tile_count, width, 2, GRID * GRID)
    return lax.all_to_all(partial_value, "tm", split_axis=0, concat_axis=1, tiled=True).astype(F32)


def solution(mesh):
    placed = (P("chan", "tm", None), P(), P(), P(), P(), P())
    return jax.shard_map(
        body, mesh=mesh, in_specs=placed, out_specs=P("tm", "chan", None, None), check_vma=False
    )
```
